128 devices in a mesh: dp: 16 (over z, y), fsdp: 8 (over x, core).
Axes of the slice: x: 4, y: 4, z: 4, core: 2. Of those that a mesh axis runs over, the one named last changes fastest.
Arguments:
- queries: bfloat16 [49152, 2048], P(('dp', 'fsdp')), may hold values from -16 to 16
- passages: bfloat16 [49152, 2048], P(('dp', 'fsdp')), may hold values from -16 to 16
- weight: bfloat16 [2048, 2048], P('fsdp'), may hold values from -0.125 to 0.125
- bank: bfloat16 [1024, 128, 2048], P(('dp', 'fsdp')), may hold values from -6 to 6
- neg_ids: int32 [128, 16], P(('dp', 'fsdp')), may hold values from 0 to 1023, as said below
- block_home: int32 [1024], replicated, may hold values from 0 to 1023, as said below
Outputs:
- loss: float32 [], replicated
- grad_weight: float32 [2048, 2048], P(('dp', 'fsdp'))
- grad_queries: bfloat16 [49152, 2048], P(('dp', 'fsdp'))
- grad_passages: bfloat16 [49152, 2048], P(('dp', 'fsdp'))
The draws below stay inside these ranges and needn't reach their ends.
Inputs may be any that keep to these rules, and one draw needn't show every extreme that they name: `block_home`: A permutation of the slots; block b is held on a device whose fsdp index is b % 8. `neg_ids`: A group's 16 blocks are distinct and all held on devices of the group's own fsdp index; at most 2 of them on one device, and in every group some device holds exactly 2; in each fsdp index one device holds 2 of every group's blocks.
All inputs are finite; a program needn't handle non-finite values.
Results may differ from the reference program's by a relative error of at most 0.012.
The reference program's roundings to bfloat16 on the way (of `negs` and `grad_s`) count: a program that leaves them out, or rounds other values in their place, can miss the bound.
Values may be sent and summed in bfloat16 or wider, within the bound.
A program may use at most 128 MiB of HBM per device.

```python
import math
import jax
import jax.numpy as jnp
from jax import lax

KIN = 2048
EMBED_WIDTH = 2048
QDEV = 384
BLK = 128
NEG = 16
NB_DEV = 8
QTOT = 49152
NBLK = 1024
N_DP = 16
N_FSDP = 8
DEVICES = 128


def home_tables(key):
    column = N_DP * NB_DEV
    keys = jax.random.split(key, N_FSDP)
    sorted_orders = jax.vmap(lambda one: jax.random.permutation(one, column))(keys)
    lanes = jnp.arange(N_FSDP)[:, None]
    slots = (sorted_orders // NB_DEV * N_FSDP + lanes) * NB_DEV + sorted_orders % NB_DEV
    home = slots.T.reshape(NBLK).astype(jnp.int32)
    inverse = jnp.argsort(sorted_orders, axis=1, stable=True).astype(jnp.int32)
    return (home, inverse)


def draw_block_home(key, part):
    home, inverse = home_tables(key)
    return home


def draw_neg_ids(key, part):
    home, inverse = home_tables(key)
    key = jax.random.fold_in(key, 11)
    key_hot, key_perm, key_double, key_local = jax.random.split(key, 4)
    device_index = jnp.arange(DEVICES)
    lane = device_index % N_FSDP
    hot = jax.random.randint(key_hot, (N_FSDP,), 0, N_DP)[lane]
    others = jax.vmap(lambda one: jax.random.permutation(one, N_DP - 1))(jax.random.split(key_perm, DEVICES))
    rest = NEG - 2
    low = max(rest - (N_DP - 1), 0)
    doubled = jax.random.randint(key_double, (DEVICES,), low, rest // 2 + 1)
    steps = jnp.arange(rest)[None, :]
    paired = steps < 2 * doubled[:, None]
    where_at = jnp.where(paired, steps // 2, steps - doubled[:, None])
    picked = jnp.take_along_axis(others, where_at, axis=1)
    owners = jnp.concatenate([hot[:, None], hot[:, None], (hot[:, None] + 1 + picked) % N_DP], axis=1)
    copies = jnp.concatenate([jnp.zeros((DEVICES, 1), jnp.int32), jnp.ones((DEVICES, 1), jnp.int32), jnp.where(paired, steps % 2, 0).astype(jnp.int32)], axis=1)
    local_orders = jax.vmap(lambda one: jax.random.permutation(one, NB_DEV))(jax.random.split(key_local, DEVICES * N_DP))
    local_orders = local_orders.reshape(DEVICES, N_DP, NB_DEV)
    local = local_orders[device_index[:, None], owners, copies]
    column_slot = owners * NB_DEV + local
    ids = inverse[lane[:, None], column_slot] * N_FSDP + lane[:, None]
    return ids.astype(jnp.int32)


def group_ramp(low, high):
    group = (jnp.arange(QTOT) // QDEV).astype(jnp.float32)
    return (low * (high / low) ** (group / (DEVICES - 1)))[:, None]


def draw_queries(key, part):
    key = jax.random.fold_in(key, 5)
    rows = jnp.clip(jax.random.normal(key, (QTOT, KIN), jnp.float32), -6.0, 6.0)
    return (rows * group_ramp(0.5, 2.5)).astype(jnp.bfloat16)


def draw_passages(key, part):
    key = jax.random.fold_in(key, 6)
    return jnp.clip(jax.random.normal(key, (QTOT, KIN), jnp.float32), -6.0, 6.0).astype(jnp.bfloat16)


def block_levels(own_key, shape, cuts, least, largest):
    loudness = 1.0
    for dim, parts in cuts:
        heights = jax.random.uniform(jax.random.fold_in(jax.random.fold_in(own_key, 6), dim), (parts,), jnp.float32, least / len(cuts), largest / len(cuts))
        loudness = loudness * jnp.repeat(jnp.exp(heights), shape[dim] // parts).reshape((-1,) + (1,) * (len(shape) - 1 - dim))
    return loudness


def normal_values(own_key, dims, scale, reach, cuts=(), kind=jnp.bfloat16):
    level = block_levels(own_key, dims, cuts, -0.22, 0.18) if cuts else 1.0
    result = jax.random.normal(own_key, dims, jnp.float32) * scale * level
    return jnp.minimum(jnp.maximum(result, -reach), reach).astype(kind)


def setup_inputs(seed: int = 0) -> dict:
    key_of = jax.random.split(jax.random.key(seed), 7)
    return {
        "queries": draw_queries(jax.random.fold_in(key_of[6], 71), 0),
        "passages": draw_passages(jax.random.fold_in(key_of[6], 71), 0),
        "weight": normal_values(key_of[2], (KIN, EMBED_WIDTH), KIN ** -0.5, 0.125, ((0, 8),)),
        "bank": normal_values(key_of[3], (NBLK, BLK, EMBED_WIDTH), 1.0, 6.0, ((0, 128),)),
        "neg_ids": draw_neg_ids(jax.random.fold_in(key_of[6], 71), 0),
        "block_home": draw_block_home(jax.random.fold_in(key_of[6], 71), 0),
    }


SOFTMAX_TEMPER = 0.25

def reference(queries, passages, weight, bank, neg_ids, block_home):
    logit_scale = 1.0 / (SOFTMAX_TEMPER * math.sqrt(EMBED_WIDTH))
    emb_q = jnp.dot(queries, weight, preferred_element_type=jnp.float32).astype(jnp.bfloat16)
    emb_p = jnp.dot(passages, weight, preferred_element_type=jnp.float32).astype(jnp.bfloat16)
    group_q = emb_q.reshape(DEVICES, QDEV, EMBED_WIDTH)
    group_p = emb_p.reshape(DEVICES, QDEV, EMBED_WIDTH)
    slots = block_home[neg_ids].astype(jnp.int32)
    target = jnp.concatenate([jnp.eye(QDEV, dtype=jnp.float32), jnp.zeros((QDEV, NEG * BLK), jnp.float32)], axis=1)

    def group(inputs):
        q_rows, p_rows, slot_row = inputs
        negs = bank[slot_row].reshape(NEG * BLK, EMBED_WIDTH)
        inner = jnp.dot(q_rows, p_rows.T, preferred_element_type=jnp.float32) * logit_scale
        outer = jnp.dot(q_rows, negs.T, preferred_element_type=jnp.float32) * logit_scale
        scores = jnp.concatenate([inner, outer], axis=1)
        top = lax.optimization_barrier(jnp.max(scores, axis=1, keepdims=True))
        expo = jnp.exp(scores - top)
        total = lax.optimization_barrier(jnp.sum(expo, axis=1, keepdims=True))
        lse = top[:, 0] + jnp.log(total[:, 0])
        loss_sum = jnp.sum(lse - jnp.diagonal(inner))
        grad_s = ((expo / total - target) * logit_scale).astype(jnp.bfloat16)
        grad_in = grad_s[:, :QDEV]
        grad_out = grad_s[:, QDEV:]
        query_gradient = (jnp.dot(grad_in, p_rows, preferred_element_type=jnp.float32) + jnp.dot(grad_out, negs, preferred_element_type=jnp.float32)).astype(jnp.bfloat16)
        grad_p = jnp.dot(grad_in.T, q_rows, preferred_element_type=jnp.float32).astype(jnp.bfloat16)
        return (loss_sum, query_gradient, grad_p)
    losses, query_gradient, grad_p = lax.map(group, (group_q, group_p, slots))
    loss = jnp.sum(losses) / QTOT
    query_gradient = query_gradient.reshape(QTOT, EMBED_WIDTH)
    grad_p = grad_p.reshape(QTOT, EMBED_WIDTH)
    grad_weight = jnp.dot(queries.T, query_gradient, preferred_element_type=jnp.float32) + jnp.dot(passages.T, grad_p, preferred_element_type=jnp.float32)
    grad_queries = jnp.dot(query_gradient, weight.T, preferred_element_type=jnp.float32).astype(jnp.bfloat16)
    grad_passages = jnp.dot(grad_p, weight.T, preferred_element_type=jnp.float32).astype(jnp.bfloat16)
    return (loss, grad_weight, grad_queries, grad_passages)
```

```python
import math

import jax
import jax.numpy as jnp
from jax import lax
from jax.experimental import pallas as pl
from jax.experimental.pallas import tpu as pltpu
from jax.sharding import PartitionSpec as P

CAP = 2


SOFTMAX_TEMPER = 0.25

MESH = pl.DeviceIdType.MESH
RING = 4
ROWS = 16
PARTS = (
    (0, 768, 384, (2, 1, 0)),
    (768, 640, 384, (1, 0, 2)),
    (1408, 640, 384, (0, 2, 1)),
)


def position():
    dp = lax.axis_index("dp")
    fsdp = lax.axis_index("fsdp")
    return (lax.div(dp, RING), lax.rem(dp, RING), lax.div(fsdp, 2)), lax.rem(fsdp, 2)


def device(coords, core):
    return (coords[0] * RING + coords[1], coords[2] * 2 + core)


def shifted(coords, axis, by):
    moved = list(coords)
    moved[axis] = lax.rem(coords[axis] + by + RING, RING)
    return tuple(moved)


def greet(targets):
    barrier = pltpu.get_barrier_semaphore()
    for target in targets:
        pl.semaphore_signal(barrier, inc=1, device_id=target, device_id_type=MESH)
    pl.semaphore_wait(barrier, len(targets))


def remote(src, dst, send, recv, target):
    return pltpu.make_async_remote_copy(
        src_ref=src, dst_ref=dst, send_sem=send, recv_sem=recv, device_id=target, device_id_type=MESH
    )


def pick(rank, spot, index, columns):
    return tuple(index if i == spot else slice(None) for i in range(rank)) + (slice(None), columns)


def reduce_kernel(share_ref, loss_ref, out_ref, total_ref, *scratch):
    coords, core = position()
    sibling = device(coords, 1 - core)
    near = [[device(shifted(coords, a, by), core) for by in (1, 3)] for a in range(3)]
    far = [device(shifted(coords, a, 2), core) for a in range(3)]
    greet([sibling] + [d for pair in near for d in pair] + far)

    count = len(PARTS)
    paired = scratch[0]
    sums = [[scratch[1 + 3 * p + k] for k in range(3)] for p in range(count)]
    base = 1 + 3 * count
    passing = [[[scratch[base + 6 * p + 2 * k + d] for d in range(2)] for k in range(3)] for p in range(count)]
    base += 6 * count
    arriving = [[scratch[base + 3 * p + k] for k in range(3)] for p in range(count)]
    base += 3 * count
    loss_buf, send0, recv0, send, recv, loss_send, loss_recv = scratch[base:]

    started = []

    def go(copy):
        copy.start()
        started.append(copy)
        return copy

    first = []
    for p, (lo, width, cut, order) in enumerate(PARTS):
        columns = pl.ds(lo, width)
        first.append(
            go(
                remote(
                    share_ref.at[:, :, :, 1 - core, :, columns],
                    paired.at[:, :, :, :, columns],
                    send0.at[p],
                    recv0.at[p],
                    sibling,
                )
            )
        )

    loss_buf[0, pl.ds(core, 1)] = loss_ref[...][None]
    pair_loss = go(
        remote(loss_buf.at[0, core], loss_buf.at[0, core], loss_send.at[0, 0], loss_recv.at[0, 0], sibling)
    )

    def loss_step(level, copies, slots):
        for copy in copies:
            copy.wait_recv()
        value = loss_buf[level, 0]
        for s in range(1, slots):
            value = value + loss_buf[level, s]
        return value

    def loss_send_axis(level, axis, value):
        mine = coords[axis]
        loss_buf[level, pl.ds(mine, 1)] = value[None]
        copies = []
        for n, target in enumerate((near[axis][0], near[axis][1], far[axis])):
            copies.append(
                go(
                    remote(
                        loss_buf.at[level, mine],
                        loss_buf.at[level, mine],
                        loss_send.at[level, n],
                        loss_recv.at[level, n],
                        target,
                    )
                )
            )
        return copies

    def halves(width, cut):
        return pl.ds(0, cut), pl.ds(cut, width - cut)

    def begin(p, k):
        lo, width, cut, order = PARTS[p]
        axis = order[k]
        rest = sorted(order[k:])
        spot, rank = rest.index(axis), len(rest)
        mine = coords[axis]
        both = halves(width, cut)
        source = sums[p][k]
        moves = {"far": [], "near": []}
        for d in range(2):
            moves["far"].append(
                go(
                    remote(
                        source.at[pick(rank, spot, lax.rem(mine + 2, RING), both[d])],
                        passing[p][k][d],
                        send.at[p, k, d],
                        recv.at[p, k, d],
                        near[axis][d],
                    )
                )
            )
        for d in range(2):
            by = 1 if d == 0 else 3
            moves["near"].append(
                go(
                    remote(
                        source.at[pick(rank, spot, lax.rem(mine + by, RING), both[1 - d])],
                        arriving[p][k].at[(d,) + pick(rank - 1, -1, 0, both[1 - d])],
                        send.at[p, k, 2 + d],
                        recv.at[p, k, 2 + d],
                        near[axis][d],
                    )
                )
            )
        return moves

    def relay(p, k, moves):
        lo, width, cut, order = PARTS[p]
        axis = order[k]
        rest = sorted(order[k:])
        spot, rank = rest.index(axis), len(rest)
        mine = coords[axis]
        both = halves(width, cut)
        source = sums[p][k]
        for d in range(2):
            by = 1 if d == 0 else 3
            moves["far"][d].wait_recv()
            where = pick(rank, spot, lax.rem(mine + by, RING), both[d])
            mixed = source[where].astype(jnp.float32) + passing[p][k][d][...].astype(jnp.float32)
            source[where] = mixed.astype(jnp.bfloat16)
            moves["near"].append(
                go(
                    remote(
                        source.at[where],
                        arriving[p][k].at[(d,) + pick(rank - 1, -1, 0, both[d])],
                        send.at[p, k, 4 + d],
                        recv.at[p, k, 4 + d],
                        near[axis][d],
                    )
                )
            )

    def finish(p, k, moves):
        lo, width, cut, order = PARTS[p]
        axis = order[k]
        rest = sorted(order[k:])
        spot, rank = rest.index(axis), len(rest)
        for copy in moves["near"]:
            copy.wait_recv()
        own = sums[p][k][pick(rank, spot, coords[axis], slice(None))].astype(jnp.float32)
        done = own + arriving[p][k][0].astype(jnp.float32) + arriving[p][k][1].astype(jnp.float32)
        if k < 2:
            sums[p][k + 1][...] = done.astype(jnp.bfloat16)
        else:
            out_ref[:, pl.ds(lo, width)] = done

    moves = []
    for p, (lo, width, cut, order) in enumerate(PARTS):
        columns = pl.ds(lo, width)
        first[p].wait_recv()

        @pl.loop(0, RING)
        def _(i):
            a = share_ref[i, :, :, core, :, columns].astype(jnp.float32)
            b = paired[i, :, :, :, columns].astype(jnp.float32)
            sums[p][0][i] = (a + b).astype(jnp.bfloat16)

        moves.append(begin(p, 0))

    value = loss_step(0, [pair_loss], 2)
    for k in range(3):
        loss_copies = loss_send_axis(1 + k, k, value)
        for p in range(count):
            relay(p, k, moves[p])
        for p in range(count):
            finish(p, k, moves[p])
            if k < 2:
                moves[p] = begin(p, k + 1)
        value = loss_step(1 + k, loss_copies, RING)
    total_ref[...] = value
    for copy in started:
        copy.wait_send()


def reduce_gradient(share, loss):
    width = share.shape[1]
    share = share.reshape(RING, RING, RING, 2, ROWS, width)
    scratch = [pltpu.VMEM((RING, RING, RING, ROWS, width), jnp.bfloat16)]
    for _, columns, _, _ in PARTS:
        scratch += [pltpu.VMEM((RING,) * (3 - k) + (ROWS, columns), jnp.bfloat16) for k in range(3)]
    for _, columns, cut, _ in PARTS:
        for k in range(3):
            for part in (cut, columns - cut):
                scratch.append(pltpu.VMEM((RING,) * (2 - k) + (ROWS, part), jnp.bfloat16))
    for _, columns, _, _ in PARTS:
        scratch += [pltpu.VMEM((2,) + (RING,) * (2 - k) + (ROWS, columns), jnp.bfloat16) for k in range(3)]
    scratch += [
        pltpu.VMEM((4, RING, 8, 128), jnp.float32),
        pltpu.SemaphoreType.DMA((len(PARTS),)),
        pltpu.SemaphoreType.DMA((len(PARTS),)),
        pltpu.SemaphoreType.DMA((len(PARTS), 3, 6)),
        pltpu.SemaphoreType.DMA((len(PARTS), 3, 6)),
        pltpu.SemaphoreType.DMA((4, 3)),
        pltpu.SemaphoreType.DMA((4, 3)),
    ]
    vmem = pl.BlockSpec(memory_space=pltpu.VMEM)
    return pl.pallas_call(
        reduce_kernel,
        out_shape=(
            jax.ShapeDtypeStruct((ROWS, width), jnp.float32),
            jax.ShapeDtypeStruct((8, 128), jnp.float32),
        ),
        in_specs=[vmem, vmem],
        out_specs=(vmem, vmem),
        scratch_shapes=scratch,
        compiler_params=pltpu.CompilerParams(
            collective_id=2, has_side_effects=True, vmem_limit_bytes=48 * 1024 * 1024
        ),
        name="reduce_gradient",
    )(share, loss)


def body(queries, passages, weight, bank, neg_ids, block_home):
    count_q = queries.shape[0]
    slice_width = weight.shape[1]
    logit_scale = 1.0 / (SOFTMAX_TEMPER * math.sqrt(slice_width))
    full_weight = lax.all_gather(weight, "fsdp", axis=0, tiled=True)
    hidden = jnp.concatenate([queries, passages], axis=0)
    embedded = jnp.dot(hidden, full_weight, preferred_element_type=jnp.float32).astype(jnp.bfloat16)
    emb_q = embedded[:count_q]
    emb_p = embedded[count_q:]
    n_dp = lax.axis_size("dp")
    n_fsdp = lax.axis_size("fsdp")
    per_dev = bank.shape[0]
    block_rows = bank.shape[1]
    named = neg_ids.shape[1]
    slots = block_home[neg_ids[0]]
    owner = slots // per_dev // n_fsdp
    local = slots % per_dev
    order = jnp.arange(named)
    earlier = (owner[None, :] == owner[:, None]) & (order[None, :] < order[:, None])
    rank = jnp.sum(earlier.astype(jnp.int32), axis=1)
    peers = jnp.arange(n_dp)
    places = jnp.arange(CAP)
    hit = (owner[:, None, None] == peers[None, :, None]) & (
        rank[:, None, None] == places[None, None, :]
    )
    request = jnp.sum(jnp.where(hit, local[:, None, None] + 1, 0), axis=0) - 1
    asked = lax.all_to_all(request, "dp", split_axis=0, concat_axis=0, tiled=True)
    valid = asked >= 0
    picked = jnp.take(bank, jnp.clip(asked, 0, per_dev - 1), axis=0)
    picked = jnp.where(valid[:, :, None, None], picked, jnp.zeros_like(picked))
    replies = lax.all_to_all(picked, "dp", split_axis=0, concat_axis=0, tiled=True)
    replies = replies.reshape(n_dp * CAP, block_rows, slice_width)
    negs = jnp.take(replies, owner * CAP + rank, axis=0).reshape(named * block_rows, slice_width)
    inner = jnp.dot(emb_q, emb_p.T, preferred_element_type=jnp.float32) * logit_scale
    outer = jnp.dot(emb_q, negs.T, preferred_element_type=jnp.float32) * logit_scale
    scores = jnp.concatenate([inner, outer], axis=1)
    top = jnp.max(scores, axis=1, keepdims=True)
    expo = jnp.exp(scores - top)
    total = jnp.sum(expo, axis=1, keepdims=True)
    lse = top[:, 0] + jnp.log(total[:, 0])
    loss_local = jnp.sum(lse - jnp.diagonal(inner))
    target = jnp.concatenate(
        [
            jnp.eye(count_q, dtype=jnp.float32),
            jnp.zeros((count_q, named * block_rows), jnp.float32),
        ],
        axis=1,
    )
    grad_s = ((expo / total - target) * logit_scale).astype(jnp.bfloat16)
    grad_in = grad_s[:, :count_q]
    grad_out = grad_s[:, count_q:]
    query_gradient = (
        jnp.dot(grad_in, emb_p, preferred_element_type=jnp.float32)
        + jnp.dot(grad_out, negs, preferred_element_type=jnp.float32)
    ).astype(jnp.bfloat16)
    grad_p = lax.dot_general(
        grad_in, emb_q, (((0,), (0,)), ((), ())), preferred_element_type=jnp.float32
    ).astype(jnp.bfloat16)
    grad_rows = jnp.concatenate([query_gradient, grad_p], axis=0)
    back = lax.dot_general(
        grad_rows, full_weight, (((1,), (1,)), ((), ())), preferred_element_type=jnp.float32
    ).astype(jnp.bfloat16)
    devices_all = n_dp * n_fsdp
    share = lax.dot_general(
        hidden, grad_rows, (((0,), (0,)), ((), ())), preferred_element_type=jnp.float32
    ).astype(jnp.bfloat16)
    grad_weight, losses = reduce_gradient(share, jnp.full((8, 128), loss_local, jnp.float32))
    loss = losses[0, 0] / (count_q * devices_all)
    return (loss, grad_weight, back[:count_q], back[count_q:])


def solution(mesh):
    return jax.shard_map(
        body,
        mesh=mesh,
        in_specs=(
            P(("dp", "fsdp"), None),
            P(("dp", "fsdp"), None),
            P("fsdp", None),
            P(("dp", "fsdp"), None, None),
            P(("dp", "fsdp"), None),
            P(),
        ),
        out_specs=(P(), P(("dp", "fsdp"), None), P(("dp", "fsdp"), None), P(("dp", "fsdp"), None)),
        check_vma=False,
    )
```

```python
import math

import jax
import jax.numpy as jnp
from jax import lax
from jax.experimental import pallas as pl
from jax.experimental.pallas import tpu as pltpu
from jax.sharding import PartitionSpec as P

SOFTMAX_TEMPER = 0.25

MESH = pl.DeviceIdType.MESH
RING = 4
ROWS = 16
PARTS = (
    (0, 768, 384, (2, 1, 0)),
    (768, 640, 384, (1, 0, 2)),
    (1408, 640, 384, (0, 2, 1)),
)


def position():
    dp = lax.axis_index("dp")
    fsdp = lax.axis_index("fsdp")
    return (lax.div(dp, RING), lax.rem(dp, RING), lax.div(fsdp, 2)), lax.rem(fsdp, 2)


def device(coords, core):
    return (coords[0] * RING + coords[1], coords[2] * 2 + core)


def shifted(coords, axis, by):
    moved = list(coords)
    moved[axis] = lax.rem(coords[axis] + by + RING, RING)
    return tuple(moved)


def greet(targets):
    barrier = pltpu.get_barrier_semaphore()
    for target in targets:
        pl.semaphore_signal(barrier, inc=1, device_id=target, device_id_type=MESH)
    pl.semaphore_wait(barrier, len(targets))


def remote(src, dst, send, recv, target):
    return pltpu.make_async_remote_copy(
        src_ref=src, dst_ref=dst, send_sem=send, recv_sem=recv, device_id=target, device_id_type=MESH
    )


def pick(rank, spot, index, columns):
    return tuple(index if i == spot else slice(None) for i in range(rank)) + (slice(None), columns)


def reduce_kernel(share_ref, loss_ref, out_ref, total_ref, *scratch):
    coords, core = position()
    sibling = device(coords, 1 - core)
    near = [[device(shifted(coords, a, by), core) for by in (1, 3)] for a in range(3)]
    far = [device(shifted(coords, a, 2), core) for a in range(3)]
    greet([sibling] + [d for pair in near for d in pair] + far)

    count = len(PARTS)
    paired = scratch[0]
    sums = [[scratch[1 + 3 * p + k] for k in range(3)] for p in range(count)]
    base = 1 + 3 * count
    passing = [[[scratch[base + 6 * p + 2 * k + d] for d in range(2)] for k in range(3)] for p in range(count)]
    base += 6 * count
    arriving = [[scratch[base + 3 * p + k] for k in range(3)] for p in range(count)]
    base += 3 * count
    loss_buf, send0, recv0, send, recv, loss_send, loss_recv = scratch[base:]

    started = []

    def go(copy):
        copy.start()
        started.append(copy)
        return copy

    first = []
    for p, (lo, width, cut, order) in enumerate(PARTS):
        columns = pl.ds(lo, width)
        first.append(
            go(
                remote(
                    share_ref.at[:, :, :, 1 - core, :, columns],
                    paired.at[:, :, :, :, columns],
                    send0.at[p],
                    recv0.at[p],
                    sibling,
                )
            )
        )

    loss_buf[0, pl.ds(core, 1)] = loss_ref[...][None]
    pair_loss = go(
        remote(loss_buf.at[0, core], loss_buf.at[0, core], loss_send.at[0, 0], loss_recv.at[0, 0], sibling)
    )

    def loss_step(level, copies, slots):
        for copy in copies:
            copy.wait_recv()
        value = loss_buf[level, 0]
        for s in range(1, slots):
            value = value + loss_buf[level, s]
        return value

    def loss_send_axis(level, axis, value):
        mine = coords[axis]
        loss_buf[level, pl.ds(mine, 1)] = value[None]
        copies = []
        for n, target in enumerate((near[axis][0], near[axis][1], far[axis])):
            copies.append(
                go(
                    remote(
                        loss_buf.at[level, mine],
                        loss_buf.at[level, mine],
                        loss_send.at[level, n],
                        loss_recv.at[level, n],
                        target,
                    )
                )
            )
        return copies

    def halves(width, cut):
        return pl.ds(0, cut), pl.ds(cut, width - cut)

    def begin(p, k):
        lo, width, cut, order = PARTS[p]
        axis = order[k]
        rest = sorted(order[k:])
        spot, rank = rest.index(axis), len(rest)
        mine = coords[axis]
        both = halves(width, cut)
        source = sums[p][k]
        moves = {"far": [], "near": []}
        for d in range(2):
            moves["far"].append(
                go(
                    remote(
                        source.at[pick(rank, spot, lax.rem(mine + 2, RING), both[d])],
                        passing[p][k][d],
                        send.at[p, k, d],
                        recv.at[p, k, d],
                        near[axis][d],
                    )
                )
            )
        for d in range(2):
            by = 1 if d == 0 else 3
            moves["near"].append(
                go(
                    remote(
                        source.at[pick(rank, spot, lax.rem(mine + by, RING), both[1 - d])],
                        arriving[p][k].at[(d,) + pick(rank - 1, -1, 0, both[1 - d])],
                        send.at[p, k, 2 + d],
                        recv.at[p, k, 2 + d],
                        near[axis][d],
                    )
                )
            )
        return moves

    def relay(p, k, moves):
        lo, width, cut, order = PARTS[p]
        axis = order[k]
        rest = sorted(order[k:])
        spot, rank = rest.index(axis), len(rest)
        mine = coords[axis]
        both = halves(width, cut)
        source = sums[p][k]
        for d in range(2):
            by = 1 if d == 0 else 3
            moves["far"][d].wait_recv()
            where = pick(rank, spot, lax.rem(mine + by, RING), both[d])
            mixed = source[where].astype(jnp.float32) + passing[p][k][d][...].astype(jnp.float32)
            source[where] = mixed.astype(jnp.bfloat16)
            moves["near"].append(
                go(
                    remote(
                        source.at[where],
                        arriving[p][k].at[(d,) + pick(rank - 1, -1, 0, both[d])],
                        send.at[p, k, 4 + d],
                        recv.at[p, k, 4 + d],
                        near[axis][d],
                    )
                )
            )

    def finish(p, k, moves):
        lo, width, cut, order = PARTS[p]
        axis = order[k]
        rest = sorted(order[k:])
        spot, rank = rest.index(axis), len(rest)
        for copy in moves["near"]:
            copy.wait_recv()
        own = sums[p][k][pick(rank, spot, coords[axis], slice(None))].astype(jnp.float32)
        done = own + arriving[p][k][0].astype(jnp.float32) + arriving[p][k][1].astype(jnp.float32)
        if k < 2:
            sums[p][k + 1][...] = done.astype(jnp.bfloat16)
        else:
            out_ref[:, pl.ds(lo, width)] = done

    moves = []
    for p, (lo, width, cut, order) in enumerate(PARTS):
        columns = pl.ds(lo, width)
        first[p].wait_recv()

        @pl.loop(0, RING)
        def _(i):
            a = share_ref[i, :, :, core, :, columns].astype(jnp.float32)
            b = paired[i, :, :, :, columns].astype(jnp.float32)
            sums[p][0][i] = (a + b).astype(jnp.bfloat16)

        moves.append(begin(p, 0))

    value = loss_step(0, [pair_loss], 2)
    for k in range(3):
        loss_copies = loss_send_axis(1 + k, k, value)
        for p in range(count):
            relay(p, k, moves[p])
        for p in range(count):
            finish(p, k, moves[p])
            if k < 2:
                moves[p] = begin(p, k + 1)
        value = loss_step(1 + k, loss_copies, RING)
    total_ref[...] = value
    for copy in started:
        copy.wait_send()


def reduce_gradient(share, loss):
    width = share.shape[1]
    share = share.reshape(RING, RING, RING, 2, ROWS, width)
    scratch = [pltpu.VMEM((RING, RING, RING, ROWS, width), jnp.bfloat16)]
    for _, columns, _, _ in PARTS:
        scratch += [pltpu.VMEM((RING,) * (3 - k) + (ROWS, columns), jnp.bfloat16) for k in range(3)]
    for _, columns, cut, _ in PARTS:
        for k in range(3):
            for part in (cut, columns - cut):
                scratch.append(pltpu.VMEM((RING,) * (2 - k) + (ROWS, part), jnp.bfloat16))
    for _, columns, _, _ in PARTS:
        scratch += [pltpu.VMEM((2,) + (RING,) * (2 - k) + (ROWS, columns), jnp.bfloat16) for k in range(3)]
    scratch += [
        pltpu.VMEM((4, RING, 8, 128), jnp.float32),
        pltpu.SemaphoreType.DMA((len(PARTS),)),
        pltpu.SemaphoreType.DMA((len(PARTS),)),
        pltpu.SemaphoreType.DMA((len(PARTS), 3, 6)),
        pltpu.SemaphoreType.DMA((len(PARTS), 3, 6)),
        pltpu.SemaphoreType.DMA((4, 3)),
        pltpu.SemaphoreType.DMA((4, 3)),
    ]
    vmem = pl.BlockSpec(memory_space=pltpu.VMEM)
    return pl.pallas_call(
        reduce_kernel,
        out_shape=(
            jax.ShapeDtypeStruct((ROWS, width), jnp.float32),
            jax.ShapeDtypeStruct((8, 128), jnp.float32),
        ),
        in_specs=[vmem, vmem],
        out_specs=(vmem, vmem),
        scratch_shapes=scratch,
        compiler_params=pltpu.CompilerParams(
            collective_id=2, has_side_effects=True, vmem_limit_bytes=48 * 1024 * 1024
        ),
        name="reduce_gradient",
    )(share, loss)


def ring_position():
    coords, core = position()
    r = coords[0] + core * (coords[1] - coords[0])
    q = coords[1] + core * (coords[0] - coords[1])
    return r, q, coords[2], core


def ring_device(r, q, x, core):
    r = lax.rem(r + RING, RING)
    q = lax.rem(q + RING, RING)
    x = lax.rem(x + RING, RING)
    return (r * (RING - (RING - 1) * core) + q * (1 + (RING - 1) * core), x * 2 + core)


def gather_kernel(
    q_ref, p_ref, w_ref, bank_ref, list_ref,
    blocks_ref, allq_ref, embp_ref, full_ref, lists_ref,
    w_buf, h_buf, acc, embq, embp, list_buf, local_sem, send, recv,
):
    r, q, x, core = ring_position()
    sibling = ring_device(r, q, x, 1 - core)
    ring = [ring_device(r + by, q, x, core) for by in (1, -1)]
    row = [ring_device(r, q + by, x, core) for by in (1, -1)]
    row_far = ring_device(r, q + 2, x, core)
    line = [ring_device(r, q, x + by, core) for by in (1, -1)]
    rows = q_ref.shape[0]
    depth = w_ref.shape[0]
    many = bank_ref.shape[0]
    own = x * 2 + core
    other = x * 2 + 1 - core

    def wrap(v):
        return lax.rem(v + RING, RING)

    local = []

    def keep(src, dst):
        copy = pltpu.make_async_copy(src, dst, local_sem.at[len(local)])
        copy.start()
        local.append(copy)
        return copy

    started = []

    def go(src, dst, target):
        n = len(started)
        copy = remote(src, dst, send.at[n], recv.at[n], target)
        copy.start()
        started.append(copy)
        return copy

    take_q = keep(q_ref, h_buf.at[pl.ds(0, rows)])
    take_p = keep(p_ref, h_buf.at[pl.ds(rows, rows)])
    take_w = keep(w_ref, w_buf.at[own])
    greet([sibling] + ring + row + [row_far] + line)

    cut_w = (pl.ds(0, depth // 2), pl.ds(depth // 2, depth // 2))
    cut_b = (pl.ds(0, many // 2), pl.ds(many // 2, many // 2))
    cut_q = (pl.ds(0, rows // 2), pl.ds(rows // 2, rows // 2))

    w_pair = go(w_ref, w_buf.at[own], sibling)
    w_near = [None, None]
    b_near = [None, None]
    for d in range(2):
        w_near[d] = [go(w_ref.at[cut_w[h]], w_buf.at[own, cut_w[h]], line[d]) for h in (d, 1 - d)]
    for d in range(2):
        b_near[d] = [go(bank_ref.at[cut_b[h]], blocks_ref.at[r, cut_b[h]], ring[d]) for h in (d, 1 - d)]
    list_copies = [
        go(list_ref.at[wrap(q + by)], list_buf.at[q], target) for by, target in ((1, row[0]), (-1, row[1]), (2, row_far))
    ]
    list_buf[pl.ds(q, 1)] = list_ref[pl.ds(q, 1)]
    keep_b = keep(bank_ref, blocks_ref.at[r])

    def multiply(part, first=False):
        @pl.loop(0, acc.shape[1] // 512)
        def _(n):
            columns = pl.ds(pl.multiple_of(n * 512, 512), 512)
            term = jnp.dot(
                h_buf[:, pl.ds(pl.multiple_of(part * depth, depth), depth)],
                w_buf[part, :, columns],
                preferred_element_type=jnp.float32,
            )
            if first:
                acc[:, columns] = term
            else:
                acc[:, columns] += term

    take_q.wait()
    take_p.wait()
    take_w.wait()
    multiply(own, True)
    w_pair.wait_recv()
    multiply(other)

    across = []
    w_far = [None, None]
    for n in range(2):
        for d in range(2):
            h = d if n == 0 else 1 - d
            came = wrap(x - 1 + 2 * d) * 2 + core
            w_near[d][n].wait_recv()
            if n == 0:
                w_far[d] = go(w_buf.at[came, cut_w[h]], w_buf.at[came, cut_w[h]], line[d])
            across.append(go(w_buf.at[came, cut_w[h]], w_buf.at[came, cut_w[h]], sibling))
    multiply(wrap(x - 1) * 2 + core)
    multiply(wrap(x + 1) * 2 + core)
    b_far = [None, None]
    for d in range(2):
        came = wrap(r - 1 + 2 * d)
        b_near[d][0].wait_recv()
        b_far[d] = go(blocks_ref.at[came, cut_b[d]], blocks_ref.at[came, cut_b[d]], ring[d])
    for copy in across:
        copy.wait_recv()
    multiply(wrap(x - 1) * 2 + 1 - core)
    multiply(wrap(x + 1) * 2 + 1 - core)
    across = []
    last = wrap(x + 2) * 2
    for d in range(2):
        w_far[d].wait_recv()
        across.append(go(w_buf.at[last + core, cut_w[d]], w_buf.at[last + core, cut_w[d]], sibling))
    multiply(last + core)
    for copy in across:
        copy.wait_recv()
    multiply(last + 1 - core)

    embq[...] = acc[pl.ds(0, rows)].astype(jnp.bfloat16)
    q_near = [None, None]
    for d in range(2):
        q_near[d] = [go(embq.at[cut_q[h]], allq_ref.at[q, cut_q[h]], row[d]) for h in (d, 1 - d)]
    keep(embq, allq_ref.at[q])
    embp[...] = acc[pl.ds(rows, rows)].astype(jnp.bfloat16)
    keep(embp, embp_ref)
    keep(w_buf, full_ref)
    for copy in list_copies:
        copy.wait_recv()
    lists_ref[...] = list_buf[...]
    q_far = [None, None]
    for d in range(2):
        came = wrap(q - 1 + 2 * d)
        q_near[d][0].wait_recv()
        q_far[d] = go(allq_ref.at[came, cut_q[d]], allq_ref.at[came, cut_q[d]], row[d])
    for d in range(2):
        b_near[d][1].wait_recv()
        b_far[d].wait_recv()
        q_near[d][1].wait_recv()
        q_far[d].wait_recv()
    for copy in local[3:]:
        copy.wait()
    for copy in started:
        copy.wait_send()


def gather_and_embed(queries, passages, weight, bank, lists):
    rows, features = queries.shape
    depth, width = weight.shape
    parts = features // depth
    many, block_rows = bank.shape[:2]
    anywhere = pl.BlockSpec(memory_space=pl.ANY)
    vmem = pl.BlockSpec(memory_space=pltpu.VMEM)
    return pl.pallas_call(
        gather_kernel,
        out_shape=(
            jax.ShapeDtypeStruct((RING, many, block_rows, width), jnp.bfloat16),
            jax.ShapeDtypeStruct((RING, rows, width), jnp.bfloat16),
            jax.ShapeDtypeStruct((rows, width), jnp.bfloat16),
            jax.ShapeDtypeStruct((parts, depth, width), jnp.bfloat16),
            jax.ShapeDtypeStruct(lists.shape, jnp.int32),
        ),
        in_specs=[anywhere] * 4 + [vmem],
        out_specs=(anywhere,) * 4 + (vmem,),
        scratch_shapes=[
            pltpu.VMEM((parts, depth, width), jnp.bfloat16),
            pltpu.VMEM((2 * rows, features), jnp.bfloat16),
            pltpu.VMEM((2 * rows, width), jnp.float32),
            pltpu.VMEM((rows, width), jnp.bfloat16),
            pltpu.VMEM((rows, width), jnp.bfloat16),
            pltpu.VMEM(lists.shape, jnp.int32),
            pltpu.SemaphoreType.DMA((7,)),
            pltpu.SemaphoreType.DMA((28,)),
            pltpu.SemaphoreType.DMA((28,)),
        ],
        compiler_params=pltpu.CompilerParams(
            collective_id=0, has_side_effects=True, vmem_limit_bytes=40 * 1024 * 1024
        ),
        name="gather_and_embed",
    )(queries, passages, weight, bank, lists)


NONE = -1e30


def partial_kernel(
    scale, allq_ref, blocks_ref, embp_ref, index_ref, list_ref,
    grad_ref, loss_ref,
    q_buf, x_buf, p_buf, named, prob, score, mixed, own_mixed,
    far_out, near_out, passing, arriving,
    far_stat, near_stat, pass_stat, arrive_stat, arrive_far, local_sem, send, recv,
):
    r, q, x, core = ring_position()
    row = [ring_device(r, q + by, x, core) for by in (1, -1)]
    rows, width = p_buf.shape
    places = list_ref.shape[1]
    half = width // 2
    sides = (pl.ds(0, half), pl.ds(half, half))

    take = [
        pltpu.make_async_copy(allq_ref, q_buf, local_sem.at[0]),
        pltpu.make_async_copy(blocks_ref, x_buf, local_sem.at[1]),
        pltpu.make_async_copy(embp_ref, p_buf, local_sem.at[2]),
    ]
    for copy in take:
        copy.start()
    greet(row)
    for copy in take:
        copy.wait()

    def wrap(v):
        return lax.rem(v + RING, RING)

    started = []

    def go(src, dst, target):
        n = len(started)
        copy = remote(src, dst, send.at[n], recv.at[n], target)
        copy.start()
        started.append(copy)
        return copy

    eye = lax.broadcasted_iota(jnp.int32, (128, 128), 0) == lax.broadcasted_iota(jnp.int32, (128, 128), 1)

    def pack(stat, m, l):
        for i in range(rows // 128):
            for n, value in ((0, m), (rows // 128, l)):
                part = jnp.where(eye, value[i * 128 : (i + 1) * 128], 0.0)
                stat[pl.ds(n + i, 1)] = jnp.sum(part, axis=0, keepdims=True)

    def unpack(stat, n):
        parts = []
        for i in range(rows // 128):
            line = stat[pl.ds(n * (rows // 128) + i, 1)]
            parts.append(jnp.sum(jnp.where(eye, line, 0.0), axis=1, keepdims=True))
        return jnp.concatenate(parts, axis=0)

    def group(g, result):
        @pl.loop(0, places)
        def _(k):
            block = jnp.maximum(index_ref[g, k, 0], 0)
            named[pl.ds(pl.multiple_of(k * 128, 128), 128)] = x_buf[block]

        @pl.loop(0, places // 2)
        def _(n):
            part = pl.ds(pl.multiple_of(n * 256, 256), 256)
            score[:, part] = scale * lax.dot_general(
                q_buf[g], named[part], (((1,), (1,)), ((), ())), preferred_element_type=jnp.float32
            )

        top = jnp.full((rows, 128), NONE, jnp.float32)
        for k in range(places):
            valid = list_ref[g, pl.ds(k, 1)] >= 0
            top = jnp.maximum(top, jnp.where(valid, score[:, k * 128 : (k + 1) * 128], NONE))
        m = jnp.max(top, axis=1, keepdims=True)
        total = jnp.zeros((rows, 128), jnp.float32)
        for k in range(places):
            valid = list_ref[g, pl.ds(k, 1)] >= 0
            e = jnp.where(valid, jnp.exp(score[:, k * 128 : (k + 1) * 128] - m), 0.0)
            total = total + e
            prob[:, k * 128 : (k + 1) * 128] = e.astype(jnp.bfloat16)
        l = jnp.sum(total, axis=1, keepdims=True)

        @pl.loop(0, width // 512)
        def _(n):
            part = pl.ds(pl.multiple_of(n * 512, 512), 512)
            result[:, part] = jnp.dot(prob[...], named[:, part], preferred_element_type=jnp.float32)

        return m, l

    m, l = group(wrap(q + 2), mixed)
    pack(far_stat, m, l)
    far = []
    for d in range(2):
        far_out[d] = mixed[:, sides[d]].astype(jnp.bfloat16)
        far.append(
            (go(far_out.at[d], passing.at[d], row[d]), go(far_stat, pass_stat.at[d], row[d]))
        )
    near = []
    for d in range(2):
        m, l = group(wrap(q + 1 - 2 * d), mixed)
        pack(near_stat.at[d], m, l)
        for copy in far[d]:
            copy.wait_recv()
        m_far = unpack(pass_stat.at[d], 0)
        both = jnp.maximum(m, m_far)
        joined = mixed[:, sides[d]] * jnp.exp(m - both) + passing[d].astype(jnp.float32) * jnp.exp(m_far - both)
        near_out[d, :, sides[d]] = joined.astype(jnp.bfloat16)
        near_out[d, :, sides[1 - d]] = mixed[:, sides[1 - d]].astype(jnp.bfloat16)
        near.append(go(near_out.at[d], arriving.at[d], row[d]))
        near.append(go(near_stat.at[d], arrive_stat.at[d], row[d]))
        if d == 0:
            near.append(go(pass_stat.at[0], arrive_far, row[0]))

    m_own, l_own = group(q, own_mixed)
    inner = scale * lax.dot_general(
        q_buf[q], p_buf[...], (((1,), (1,)), ((), ())), preferred_element_type=jnp.float32
    )
    m_in = jnp.max(inner, axis=1, keepdims=True)
    l_in = jnp.sum(jnp.exp(inner - m_in), axis=1, keepdims=True)
    diagonal = lax.broadcasted_iota(jnp.int32, inner.shape, 0) == lax.broadcasted_iota(jnp.int32, inner.shape, 1)
    positive = jnp.sum(jnp.where(diagonal, inner, 0.0), axis=1, keepdims=True)

    for copy in near:
        copy.wait_recv()
    m_before, l_before = unpack(arrive_stat.at[0], 0), unpack(arrive_stat.at[0], 1)
    m_after, l_after = unpack(arrive_stat.at[1], 0), unpack(arrive_stat.at[1], 1)
    m_far, l_far = unpack(arrive_far, 0), unpack(arrive_far, 1)
    m = m_in
    for value in (m_own, m_before, m_after, m_far):
        m = jnp.maximum(m, value)
    total = l_in * jnp.exp(m_in - m)
    for part_m, part_l in ((m_own, l_own), (m_before, l_before), (m_after, l_after), (m_far, l_far)):
        total = total + part_l * jnp.exp(part_m - m)
    losses = m + jnp.log(total) - positive
    loss_ref[...] = jnp.broadcast_to(jnp.sum(losses, axis=0, keepdims=True), loss_ref.shape)
    target = jnp.where(diagonal, 1.0, 0.0)
    grad_full = (jnp.exp(inner - m) / total - target) * scale
    grad_in = grad_full.astype(jnp.bfloat16)
    by_own = jnp.exp(m_own - m) * (scale / total)
    by_before = (
        jnp.exp(jnp.maximum(m_before, m_far) - m) * (scale / total),
        jnp.exp(m_before - m) * (scale / total),
    )
    by_after = (
        jnp.exp(m_after - m) * (scale / total),
        jnp.exp(jnp.maximum(m_after, m_far) - m) * (scale / total),
    )
    for n in range(width // 512):
        part = pl.ds(n * 512, 512)
        side = n * 512 // half
        value = jnp.dot(grad_in, p_buf[:, part], preferred_element_type=jnp.float32)
        value = value + own_mixed[:, part] * by_own
        value = value + arriving[0, :, part].astype(jnp.float32) * by_before[side]
        value = value + arriving[1, :, part].astype(jnp.float32) * by_after[side]
        grad_ref[pl.ds(0, rows), part] = value.astype(jnp.bfloat16)
    turned = grad_full.T.astype(jnp.bfloat16)
    for n in range(width // 512):
        part = pl.ds(n * 512, 512)
        value = jnp.dot(turned, q_buf[q, :, part], preferred_element_type=jnp.float32)
        grad_ref[pl.ds(rows, rows), part] = value.astype(jnp.bfloat16)
    for copy in started:
        copy.wait_send()


def embedding_gradients(scale, all_q, blocks, emb_p, lists):
    rows, width = emb_p.shape
    count, block_rows = blocks.shape[0] * blocks.shape[1], blocks.shape[2]
    blocks = blocks.reshape(count, block_rows, width)
    places = lists.shape[1]
    anywhere = pl.BlockSpec(memory_space=pl.ANY)
    vmem = pl.BlockSpec(memory_space=pltpu.VMEM)
    bf16, f32 = jnp.bfloat16, jnp.float32
    return pl.pallas_call(
        lambda *refs: partial_kernel(scale, *refs),
        out_shape=(
            jax.ShapeDtypeStruct((2 * rows, width), bf16),
            jax.ShapeDtypeStruct((8, 128), f32),
        ),
        in_specs=[anywhere] * 3 + [pl.BlockSpec(memory_space=pltpu.SMEM), vmem],
        out_specs=(vmem, vmem),
        scratch_shapes=[
            pltpu.VMEM(all_q.shape, bf16),
            pltpu.VMEM(blocks.shape, bf16),
            pltpu.VMEM((rows, width), bf16),
            pltpu.VMEM((places * block_rows, width), bf16),
            pltpu.VMEM((rows, places * block_rows), bf16),
            pltpu.VMEM((rows, places * block_rows), f32),
            pltpu.VMEM((rows, width), f32),
            pltpu.VMEM((rows, width), f32),
            pltpu.VMEM((2, rows, width // 2), bf16),
            pltpu.VMEM((2, rows, width), bf16),
            pltpu.VMEM((2, rows, width // 2), bf16),
            pltpu.VMEM((2, rows, width), bf16),
            pltpu.VMEM((8, 128), f32),
            pltpu.VMEM((2, 8, 128), f32),
            pltpu.VMEM((2, 8, 128), f32),
            pltpu.VMEM((2, 8, 128), f32),
            pltpu.VMEM((8, 128), f32),
            pltpu.SemaphoreType.DMA((3,)),
            pltpu.SemaphoreType.DMA((9,)),
            pltpu.SemaphoreType.DMA((9,)),
        ],
        compiler_params=pltpu.CompilerParams(
            collective_id=1, has_side_effects=True, vmem_limit_bytes=60 * 1024 * 1024
        ),
        name="embedding_gradients",
    )(all_q, blocks, emb_p, lists, lists)


def body(queries, passages, weight, bank, neg_ids, block_home):
    count_q = queries.shape[0]
    features, slice_width = queries.shape[1], weight.shape[1]
    logit_scale = 1.0 / (SOFTMAX_TEMPER * math.sqrt(slice_width))
    n_dp = lax.axis_size("dp")
    n_fsdp = lax.axis_size("fsdp")
    per_dev = bank.shape[0]
    named = neg_ids.shape[1]
    core = lax.rem(lax.axis_index("fsdp"), 2)
    slots = block_home[neg_ids[0]]
    owner = slots // per_dev // n_fsdp
    local = slots % per_dev
    at_z, at_y = owner // RING, owner % RING
    on_ring = jnp.where(core == 0, at_z, at_y)
    on_row = jnp.where(core == 0, at_y, at_z)
    order = jnp.arange(named)
    earlier = (on_row[None, :] == on_row[:, None]) & (order[None, :] < order[:, None])
    rank = jnp.sum(earlier.astype(jnp.int32), axis=1)
    hit = (on_row[:, None, None] == jnp.arange(RING)[None, :, None]) & (
        rank[:, None, None] == jnp.arange(per_dev)[None, None, :]
    )
    block = on_ring * per_dev + local
    lists = jnp.sum(jnp.where(hit, block[:, None, None] + 1, 0), axis=0) - 1
    lists = jnp.broadcast_to(lists[:, :, None], lists.shape + (128,))

    blocks, all_q, emb_p, full_weight, all_lists = gather_and_embed(queries, passages, weight, bank, lists)
    full_weight = full_weight.reshape(features, slice_width)
    grad_rows, loss_local = embedding_gradients(logit_scale, all_q, blocks, emb_p, all_lists)
    share = (
        lax.dot_general(queries, grad_rows[:count_q], (((0,), (0,)), ((), ())), preferred_element_type=jnp.float32)
        + lax.dot_general(passages, grad_rows[count_q:], (((0,), (0,)), ((), ())), preferred_element_type=jnp.float32)
    ).astype(jnp.bfloat16)
    grad_weight, losses = reduce_gradient(share, loss_local)
    back = [
        lax.dot_general(
            grad_rows[i * count_q : (i + 1) * count_q],
            full_weight,
            (((1,), (1,)), ((), ())),
            preferred_element_type=jnp.float32,
        ).astype(jnp.bfloat16)
        for i in range(2)
    ]
    loss = losses[0, 0] / (count_q * n_dp * n_fsdp)
    return (loss, grad_weight, back[0], back[1])


def solution(mesh):
    return jax.shard_map(
        body,
        mesh=mesh,
        in_specs=(
            P(("dp", "fsdp"), None),
            P(("dp", "fsdp"), None),
            P("fsdp", None),
            P(("dp", "fsdp"), None, None),
            P(("dp", "fsdp"), None),
            P(),
        ),
        out_specs=(P(), P(("dp", "fsdp"), None), P(("dp", "fsdp"), None), P(("dp", "fsdp"), None)),
        check_vma=False,
    )
```

```python
import math

import jax
import jax.numpy as jnp
from jax import lax
from jax.experimental import pallas as pl
from jax.experimental.pallas import tpu as pltpu
from jax.sharding import PartitionSpec as P

SOFTMAX_TEMPER = 0.25

MESH = pl.DeviceIdType.MESH
RING = 4
BACK = ((0, 2), (2, 4), (4, 5), (5, 6), (6, 7), (7, 8))
ROWS = 16
PARTS = (
    (0, 768, 384, (2, 1, 0)),
    (768, 640, 384, (1, 0, 2)),
    (1408, 640, 384, (0, 2, 1)),
)


def position():
    dp = lax.axis_index("dp")
    fsdp = lax.axis_index("fsdp")
    return (lax.div(dp, RING), lax.rem(dp, RING), lax.div(fsdp, 2)), lax.rem(fsdp, 2)


def device(coords, core):
    return (coords[0] * RING + coords[1], coords[2] * 2 + core)


def shifted(coords, axis, by):
    moved = list(coords)
    moved[axis] = lax.rem(coords[axis] + by + RING, RING)
    return tuple(moved)


def greet(targets):
    barrier = pltpu.get_barrier_semaphore()
    for target in targets:
        pl.semaphore_signal(barrier, inc=1, device_id=target, device_id_type=MESH)
    pl.semaphore_wait(barrier, len(targets))


def remote(src, dst, send, recv, target):
    return pltpu.make_async_remote_copy(
        src_ref=src, dst_ref=dst, send_sem=send, recv_sem=recv, device_id=target, device_id_type=MESH
    )


def pick(rank, spot, index, columns):
    return tuple(index if i == spot else slice(None) for i in range(rank)) + (slice(None), columns)


def reduce_kernel(turned_ref, grad_ref, w_ref, loss_ref, out_ref, total_ref, backq_ref, backp_ref, *scratch):
    coords, core = position()
    sibling = device(coords, 1 - core)
    near = [[device(shifted(coords, a, by), core) for by in (1, 3)] for a in range(3)]
    far = [device(shifted(coords, a, 2), core) for a in range(3)]
    t_buf, w_buf, local_sem = scratch[-3:]
    scratch = scratch[:-3]
    take = [
        pltpu.make_async_copy(turned_ref, t_buf, local_sem.at[0]),
        pltpu.make_async_copy(w_ref, w_buf, local_sem.at[1]),
    ]
    for copy in take:
        copy.start()
    greet([sibling] + [d for pair in near for d in pair] + far)
    rows = backq_ref.shape[0]

    def back(lo, hi):
        @pl.loop(lo, hi)
        def _(n):
            value = lax.dot_general(
                grad_ref[...], w_buf[n], (((1,), (1,)), ((), ())), preferred_element_type=jnp.float32
            ).astype(jnp.bfloat16)
            columns = pl.ds(pl.multiple_of(n * w_buf.shape[1], 256), w_buf.shape[1])
            backq_ref[:, columns] = value[:rows]
            backp_ref[:, columns] = value[rows:]

    def share(which, i, columns):
        chunk = t_buf[which, pl.ds(pl.multiple_of(i * 256, 256), 256)]
        value = jnp.dot(chunk, grad_ref[:, columns], preferred_element_type=jnp.float32)
        return value.reshape((RING, RING, ROWS) + value.shape[1:])

    count = len(PARTS)
    paired, outgoing = scratch[:count], scratch[count : 2 * count]
    sums = [[scratch[2 * count + 3 * p + k] for k in range(3)] for p in range(count)]
    base = 5 * count
    passing = [[[scratch[base + 6 * p + 2 * k + d] for d in range(2)] for k in range(3)] for p in range(count)]
    base += 6 * count
    arriving = [[scratch[base + 3 * p + k] for k in range(3)] for p in range(count)]
    base += 3 * count
    loss_buf, send0, recv0, send, recv, loss_send, loss_recv = scratch[base:]

    started = []

    def go(copy):
        copy.start()
        started.append(copy)
        return copy

    take[0].wait()
    first = []
    for p, (lo, width, cut, order) in enumerate(PARTS):
        columns = pl.ds(lo, width)

        @pl.loop(0, RING)
        def _(i):
            outgoing[p][i] = share(1 - core, i, columns).astype(jnp.bfloat16)

        first.append(go(remote(outgoing[p], paired[p], send0.at[p], recv0.at[p], sibling)))

    loss_buf[0, pl.ds(core, 1)] = loss_ref[...][None]
    pair_loss = go(
        remote(loss_buf.at[0, core], loss_buf.at[0, core], loss_send.at[0, 0], loss_recv.at[0, 0], sibling)
    )

    def loss_step(level, copies, slots):
        for copy in copies:
            copy.wait_recv()
        value = loss_buf[level, 0]
        for s in range(1, slots):
            value = value + loss_buf[level, s]
        return value

    def loss_send_axis(level, axis, value):
        mine = coords[axis]
        loss_buf[level, pl.ds(mine, 1)] = value[None]
        copies = []
        for n, target in enumerate((near[axis][0], near[axis][1], far[axis])):
            copies.append(
                go(
                    remote(
                        loss_buf.at[level, mine],
                        loss_buf.at[level, mine],
                        loss_send.at[level, n],
                        loss_recv.at[level, n],
                        target,
                    )
                )
            )
        return copies

    def halves(width, cut):
        return pl.ds(0, cut), pl.ds(cut, width - cut)

    def begin(p, k):
        lo, width, cut, order = PARTS[p]
        axis = order[k]
        rest = sorted(order[k:])
        spot, rank = rest.index(axis), len(rest)
        mine = coords[axis]
        both = halves(width, cut)
        source = sums[p][k]
        moves = {"far": [], "near": []}
        for d in range(2):
            moves["far"].append(
                go(
                    remote(
                        source.at[pick(rank, spot, lax.rem(mine + 2, RING), both[d])],
                        passing[p][k][d],
                        send.at[p, k, d],
                        recv.at[p, k, d],
                        near[axis][d],
                    )
                )
            )
        for d in range(2):
            by = 1 if d == 0 else 3
            moves["near"].append(
                go(
                    remote(
                        source.at[pick(rank, spot, lax.rem(mine + by, RING), both[1 - d])],
                        arriving[p][k].at[(d,) + pick(rank - 1, -1, 0, both[1 - d])],
                        send.at[p, k, 2 + d],
                        recv.at[p, k, 2 + d],
                        near[axis][d],
                    )
                )
            )
        return moves

    def relay(p, k, moves):
        lo, width, cut, order = PARTS[p]
        axis = order[k]
        rest = sorted(order[k:])
        spot, rank = rest.index(axis), len(rest)
        mine = coords[axis]
        both = halves(width, cut)
        source = sums[p][k]
        for d in range(2):
            by = 1 if d == 0 else 3
            moves["far"][d].wait_recv()
            where = pick(rank, spot, lax.rem(mine + by, RING), both[d])
            mixed = source[where].astype(jnp.float32) + passing[p][k][d][...].astype(jnp.float32)
            source[where] = mixed.astype(jnp.bfloat16)
            moves["near"].append(
                go(
                    remote(
                        source.at[where],
                        arriving[p][k].at[(d,) + pick(rank - 1, -1, 0, both[d])],
                        send.at[p, k, 4 + d],
                        recv.at[p, k, 4 + d],
                        near[axis][d],
                    )
                )
            )

    def finish(p, k, moves):
        lo, width, cut, order = PARTS[p]
        axis = order[k]
        rest = sorted(order[k:])
        spot, rank = rest.index(axis), len(rest)
        for copy in moves["near"]:
            copy.wait_recv()
        own = sums[p][k][pick(rank, spot, coords[axis], slice(None))].astype(jnp.float32)
        done = own + arriving[p][k][0].astype(jnp.float32) + arriving[p][k][1].astype(jnp.float32)
        if k < 2:
            sums[p][k + 1][...] = done.astype(jnp.bfloat16)
        else:
            out_ref[:, pl.ds(lo, width)] = done

    moves = []
    for p, (lo, width, cut, order) in enumerate(PARTS):
        columns = pl.ds(lo, width)
        first[p].wait_recv()

        @pl.loop(0, RING)
        def _(i):
            value = share(core, i, columns) + paired[p][i].astype(jnp.float32)
            sums[p][0][i] = value.astype(jnp.bfloat16)

        moves.append(begin(p, 0))

    value = loss_step(0, [pair_loss], 2)
    for k in range(3):
        loss_copies = loss_send_axis(1 + k, k, value)
        if k == 0:
            take[1].wait()
        back(*BACK[2 * k])
        for p in range(count):
            relay(p, k, moves[p])
        back(*BACK[2 * k + 1])
        for p in range(count):
            finish(p, k, moves[p])
            if k < 2:
                moves[p] = begin(p, k + 1)
        value = loss_step(1 + k, loss_copies, RING)
    total_ref[...] = value
    for copy in started:
        copy.wait_send()


def reduce_gradient(turned, grad_rows, full_weight, loss):
    width = grad_rows.shape[1]
    rows = grad_rows.shape[0] // 2
    features = full_weight.shape[0] * full_weight.shape[1]
    scratch = [pltpu.VMEM((RING,) * 3 + (ROWS, columns), jnp.bfloat16) for _, columns, _, _ in PARTS] * 2
    for _, columns, _, _ in PARTS:
        scratch += [pltpu.VMEM((RING,) * (3 - k) + (ROWS, columns), jnp.bfloat16) for k in range(3)]
    for _, columns, cut, _ in PARTS:
        for k in range(3):
            for part in (cut, columns - cut):
                scratch.append(pltpu.VMEM((RING,) * (2 - k) + (ROWS, part), jnp.bfloat16))
    for _, columns, _, _ in PARTS:
        scratch += [pltpu.VMEM((2,) + (RING,) * (2 - k) + (ROWS, columns), jnp.bfloat16) for k in range(3)]
    scratch += [
        pltpu.VMEM((4, RING, 8, 128), jnp.float32),
        pltpu.SemaphoreType.DMA((len(PARTS),)),
        pltpu.SemaphoreType.DMA((len(PARTS),)),
        pltpu.SemaphoreType.DMA((len(PARTS), 3, 6)),
        pltpu.SemaphoreType.DMA((len(PARTS), 3, 6)),
        pltpu.SemaphoreType.DMA((4, 3)),
        pltpu.SemaphoreType.DMA((4, 3)),
        pltpu.VMEM(turned.shape, jnp.bfloat16),
        pltpu.VMEM(full_weight.shape, jnp.bfloat16),
        pltpu.SemaphoreType.DMA((2,)),
    ]
    hbm = pl.BlockSpec(memory_space=pltpu.HBM)
    vmem = pl.BlockSpec(memory_space=pltpu.VMEM)
    return pl.pallas_call(
        reduce_kernel,
        out_shape=(
            jax.ShapeDtypeStruct((ROWS, width), jnp.float32),
            jax.ShapeDtypeStruct((8, 128), jnp.float32),
            jax.ShapeDtypeStruct((rows, features), jnp.bfloat16),
            jax.ShapeDtypeStruct((rows, features), jnp.bfloat16),
        ),
        in_specs=[hbm, vmem, hbm, vmem],
        out_specs=(vmem,) * 4,
        scratch_shapes=scratch,
        compiler_params=pltpu.CompilerParams(
            collective_id=2, has_side_effects=True, vmem_limit_bytes=48 * 1024 * 1024
        ),
        name="reduce_gradient",
    )(turned, grad_rows, full_weight, loss)


def ring_position():
    coords, core = position()
    r = coords[0] + core * (coords[1] - coords[0])
    q = coords[1] + core * (coords[0] - coords[1])
    return r, q, coords[2], core


def ring_device(r, q, x, core):
    r = lax.rem(r + RING, RING)
    q = lax.rem(q + RING, RING)
    x = lax.rem(x + RING, RING)
    return (r * (RING - (RING - 1) * core) + q * (1 + (RING - 1) * core), x * 2 + core)


def gather_kernel(
    q_ref, p_ref, w_ref, bank_ref, list_ref,
    blocks_ref, allq_ref, embp_ref, full_ref, turned_ref, lists_ref,
    w_buf, h_buf, t_buf, acc, embq, embp, list_buf, local_sem, send, recv,
):
    r, q, x, core = ring_position()
    sibling = ring_device(q, r, x, 1 - core)
    ring = [ring_device(r + by, q, x, core) for by in (1, -1)]
    row = [ring_device(r, q + by, x, core) for by in (1, -1)]
    row_far = ring_device(r, q + 2, x, core)
    line = [ring_device(r, q, x + by, core) for by in (1, -1)]
    rows = q_ref.shape[0]
    depth = w_ref.shape[0]
    many = bank_ref.shape[0]
    own = x * 2 + core
    other = x * 2 + 1 - core

    def wrap(v):
        return lax.rem(v + RING, RING)

    local = []

    def keep(src, dst):
        copy = pltpu.make_async_copy(src, dst, local_sem.at[len(local)])
        copy.start()
        local.append(copy)
        return copy

    started = []

    def go(src, dst, target):
        n = len(started)
        copy = remote(src, dst, send.at[n], recv.at[n], target)
        copy.start()
        started.append(copy)
        return copy

    take_q = keep(q_ref, h_buf.at[pl.ds(0, rows)])
    take_p = keep(p_ref, h_buf.at[pl.ds(rows, rows)])
    take_w = keep(w_ref, w_buf.at[own])
    greet([sibling] + ring + row + [row_far] + line)

    cut_w = (pl.ds(0, depth // 2), pl.ds(depth // 2, depth // 2))
    cut_b = (pl.ds(0, many // 2), pl.ds(many // 2, many // 2))
    cut_q = (pl.ds(0, rows // 2), pl.ds(rows // 2, rows // 2))

    w_pair = go(w_ref, w_buf.at[own], sibling)
    w_near = [None, None]
    b_near = [None, None]
    for d in range(2):
        w_near[d] = [go(w_ref.at[cut_w[h]], w_buf.at[own, cut_w[h]], line[d]) for h in (d, 1 - d)]
    for d in range(2):
        b_near[d] = [go(bank_ref.at[cut_b[h]], blocks_ref.at[r, cut_b[h]], ring[d]) for h in (d, 1 - d)]
    list_copies = [
        go(list_ref.at[wrap(q + by)], list_buf.at[q], target) for by, target in ((1, row[0]), (-1, row[1]), (2, row_far))
    ]
    list_buf[pl.ds(q, 1)] = list_ref[pl.ds(q, 1)]
    keep_b = keep(bank_ref, blocks_ref.at[r])

    def multiply(part, first=False):
        @pl.loop(0, acc.shape[1] // 512)
        def _(n):
            columns = pl.ds(pl.multiple_of(n * 512, 512), 512)
            term = jnp.dot(
                h_buf[:, pl.ds(pl.multiple_of(part * depth, depth), depth)],
                w_buf[part, :, columns],
                preferred_element_type=jnp.float32,
            )
            if first:
                acc[:, columns] = term
            else:
                acc[:, columns] += term

    take_q.wait()
    take_p.wait()
    take_w.wait()
    multiply(own, True)
    w_pair.wait_recv()
    multiply(other)

    @pl.loop(0, h_buf.shape[1] // 256)
    def _(n):
        tile = h_buf[:, pl.ds(pl.multiple_of(n * 256, 256), 256)].T
        for i in range(256 // ROWS):
            place = pl.ds(pl.multiple_of(n * 128 + i // 2 * ROWS, ROWS), ROWS)
            t_buf[i % 2, place] = tile[i * ROWS : (i + 1) * ROWS]

    keep_t = keep(t_buf, turned_ref)

    across = []
    w_far = [None, None]
    for n in range(2):
        for d in range(2):
            h = d if n == 0 else 1 - d
            came = wrap(x - 1 + 2 * d) * 2 + core
            w_near[d][n].wait_recv()
            if n == 0:
                w_far[d] = go(w_buf.at[came, cut_w[h]], w_buf.at[came, cut_w[h]], line[d])
            across.append(go(w_buf.at[came, cut_w[h]], w_buf.at[came, cut_w[h]], sibling))
    multiply(wrap(x - 1) * 2 + core)
    multiply(wrap(x + 1) * 2 + core)
    b_far = [None, None]
    for d in range(2):
        came = wrap(r - 1 + 2 * d)
        b_near[d][0].wait_recv()
        b_far[d] = go(blocks_ref.at[came, cut_b[d]], blocks_ref.at[came, cut_b[d]], ring[d])
    for copy in across:
        copy.wait_recv()
    multiply(wrap(x - 1) * 2 + 1 - core)
    multiply(wrap(x + 1) * 2 + 1 - core)
    across = []
    last = wrap(x + 2) * 2
    for d in range(2):
        w_far[d].wait_recv()
        across.append(go(w_buf.at[last + core, cut_w[d]], w_buf.at[last + core, cut_w[d]], sibling))
    multiply(last + core)
    for copy in across:
        copy.wait_recv()
    multiply(last + 1 - core)

    embq[...] = acc[pl.ds(0, rows)].astype(jnp.bfloat16)
    q_near = [None, None]
    for d in range(2):
        q_near[d] = [go(embq.at[cut_q[h]], allq_ref.at[q, cut_q[h]], row[d]) for h in (d, 1 - d)]
    keep(embq, allq_ref.at[q])
    embp[...] = acc[pl.ds(rows, rows)].astype(jnp.bfloat16)
    keep(embp, embp_ref)
    keep(w_buf, full_ref)
    for copy in list_copies:
        copy.wait_recv()
    lists_ref[...] = list_buf[...]
    q_far = [None, None]
    for d in range(2):
        came = wrap(q - 1 + 2 * d)
        q_near[d][0].wait_recv()
        q_far[d] = go(allq_ref.at[came, cut_q[d]], allq_ref.at[came, cut_q[d]], row[d])
    for d in range(2):
        b_near[d][1].wait_recv()
        b_far[d].wait_recv()
        q_near[d][1].wait_recv()
        q_far[d].wait_recv()
    for copy in local[3:]:
        copy.wait()
    for copy in started:
        copy.wait_send()


def gather_and_embed(queries, passages, weight, bank, lists):
    rows, features = queries.shape
    depth, width = weight.shape
    parts = features // depth
    many, block_rows = bank.shape[:2]
    anywhere = pl.BlockSpec(memory_space=pltpu.HBM)
    vmem = pl.BlockSpec(memory_space=pltpu.VMEM)
    return pl.pallas_call(
        gather_kernel,
        out_shape=(
            jax.ShapeDtypeStruct((RING, many, block_rows, width), jnp.bfloat16),
            jax.ShapeDtypeStruct((RING, rows, width), jnp.bfloat16),
            jax.ShapeDtypeStruct((rows, width), jnp.bfloat16),
            jax.ShapeDtypeStruct((parts, depth, width), jnp.bfloat16),
            jax.ShapeDtypeStruct((2, features // 2, 2 * rows), jnp.bfloat16),
            jax.ShapeDtypeStruct(lists.shape, jnp.int32),
        ),
        in_specs=[anywhere] * 4 + [vmem],
        out_specs=(anywhere,) * 5 + (vmem,),
        scratch_shapes=[
            pltpu.VMEM((parts, depth, width), jnp.bfloat16),
            pltpu.VMEM((2 * rows, features), jnp.bfloat16),
            pltpu.VMEM((2, features // 2, 2 * rows), jnp.bfloat16),
            pltpu.VMEM((2 * rows, width), jnp.float32),
            pltpu.VMEM((rows, width), jnp.bfloat16),
            pltpu.VMEM((rows, width), jnp.bfloat16),
            pltpu.VMEM(lists.shape, jnp.int32),
            pltpu.SemaphoreType.DMA((8,)),
            pltpu.SemaphoreType.DMA((28,)),
            pltpu.SemaphoreType.DMA((28,)),
        ],
        compiler_params=pltpu.CompilerParams(
            collective_id=0, has_side_effects=True, vmem_limit_bytes=40 * 1024 * 1024
        ),
        name="gather_and_embed",
    )(queries, passages, weight, bank, lists)


NONE = -1e30


def partial_kernel(
    scale, allq_ref, blocks_ref, embp_ref, index_ref, list_ref,
    grad_ref, loss_ref,
    q_buf, x_buf, p_buf, named, prob, score, mixed, own_mixed,
    far_out, near_out, passing, arriving,
    far_stat, near_stat, pass_stat, arrive_stat, arrive_far, local_sem, send, recv,
):
    r, q, x, core = ring_position()
    row = [ring_device(r, q + by, x, core) for by in (1, -1)]
    rows, width = p_buf.shape
    places = list_ref.shape[1]
    half = width // 2
    sides = (pl.ds(0, half), pl.ds(half, half))

    take = [
        pltpu.make_async_copy(allq_ref, q_buf, local_sem.at[0]),
        pltpu.make_async_copy(blocks_ref, x_buf, local_sem.at[1]),
        pltpu.make_async_copy(embp_ref, p_buf, local_sem.at[2]),
    ]
    for copy in take:
        copy.start()
    greet(row)
    for copy in take:
        copy.wait()

    def wrap(v):
        return lax.rem(v + RING, RING)

    started = []

    def go(src, dst, target):
        n = len(started)
        copy = remote(src, dst, send.at[n], recv.at[n], target)
        copy.start()
        started.append(copy)
        return copy

    eye = lax.broadcasted_iota(jnp.int32, (128, 128), 0) == lax.broadcasted_iota(jnp.int32, (128, 128), 1)

    def pack(stat, m, l):
        for i in range(rows // 128):
            for n, value in ((0, m), (rows // 128, l)):
                part = jnp.where(eye, value[i * 128 : (i + 1) * 128], 0.0)
                stat[pl.ds(n + i, 1)] = jnp.sum(part, axis=0, keepdims=True)

    def unpack(stat, n):
        parts = []
        for i in range(rows // 128):
            line = stat[pl.ds(n * (rows // 128) + i, 1)]
            parts.append(jnp.sum(jnp.where(eye, line, 0.0), axis=1, keepdims=True))
        return jnp.concatenate(parts, axis=0)

    def group(g, result):
        @pl.loop(0, places)
        def _(k):
            block = jnp.maximum(index_ref[g, k, 0], 0)
            named[pl.ds(pl.multiple_of(k * 128, 128), 128)] = x_buf[block]

        @pl.loop(0, places // 2)
        def _(n):
            part = pl.ds(pl.multiple_of(n * 256, 256), 256)
            score[:, part] = scale * lax.dot_general(
                q_buf[g], named[part], (((1,), (1,)), ((), ())), preferred_element_type=jnp.float32
            )

        top = jnp.full((rows, 128), NONE, jnp.float32)
        for k in range(places):
            valid = list_ref[g, pl.ds(k, 1)] >= 0
            top = jnp.maximum(top, jnp.where(valid, score[:, k * 128 : (k + 1) * 128], NONE))
        m = jnp.max(top, axis=1, keepdims=True)
        total = jnp.zeros((rows, 128), jnp.float32)
        for k in range(places):
            valid = list_ref[g, pl.ds(k, 1)] >= 0
            e = jnp.where(valid, jnp.exp(score[:, k * 128 : (k + 1) * 128] - m), 0.0)
            total = total + e
            prob[:, k * 128 : (k + 1) * 128] = e.astype(jnp.bfloat16)
        l = jnp.sum(total, axis=1, keepdims=True)

        @pl.loop(0, width // 512)
        def _(n):
            part = pl.ds(pl.multiple_of(n * 512, 512), 512)
            result[:, part] = jnp.dot(prob[...], named[:, part], preferred_element_type=jnp.float32)

        return m, l

    m, l = group(wrap(q + 2), mixed)
    pack(far_stat, m, l)
    far = []
    for d in range(2):
        far_out[d] = mixed[:, sides[d]].astype(jnp.bfloat16)
        far.append(
            (go(far_out.at[d], passing.at[d], row[d]), go(far_stat, pass_stat.at[d], row[d]))
        )
    near = []
    for d in range(2):
        m, l = group(wrap(q + 1 - 2 * d), mixed)
        pack(near_stat.at[d], m, l)
        for copy in far[d]:
            copy.wait_recv()
        m_far = unpack(pass_stat.at[d], 0)
        both = jnp.maximum(m, m_far)
        joined = mixed[:, sides[d]] * jnp.exp(m - both) + passing[d].astype(jnp.float32) * jnp.exp(m_far - both)
        near_out[d, :, sides[d]] = joined.astype(jnp.bfloat16)
        near_out[d, :, sides[1 - d]] = mixed[:, sides[1 - d]].astype(jnp.bfloat16)
        near.append(go(near_out.at[d], arriving.at[d], row[d]))
        near.append(go(near_stat.at[d], arrive_stat.at[d], row[d]))
        if d == 0:
            near.append(go(pass_stat.at[0], arrive_far, row[0]))

    m_own, l_own = group(q, own_mixed)
    inner = scale * lax.dot_general(
        q_buf[q], p_buf[...], (((1,), (1,)), ((), ())), preferred_element_type=jnp.float32
    )
    m_in = jnp.max(inner, axis=1, keepdims=True)
    l_in = jnp.sum(jnp.exp(inner - m_in), axis=1, keepdims=True)
    diagonal = lax.broadcasted_iota(jnp.int32, inner.shape, 0) == lax.broadcasted_iota(jnp.int32, inner.shape, 1)
    positive = jnp.sum(jnp.where(diagonal, inner, 0.0), axis=1, keepdims=True)

    for copy in near:
        copy.wait_recv()
    m_before, l_before = unpack(arrive_stat.at[0], 0), unpack(arrive_stat.at[0], 1)
    m_after, l_after = unpack(arrive_stat.at[1], 0), unpack(arrive_stat.at[1], 1)
    m_far, l_far = unpack(arrive_far, 0), unpack(arrive_far, 1)
    m = m_in
    for value in (m_own, m_before, m_after, m_far):
        m = jnp.maximum(m, value)
    total = l_in * jnp.exp(m_in - m)
    for part_m, part_l in ((m_own, l_own), (m_before, l_before), (m_after, l_after), (m_far, l_far)):
        total = total + part_l * jnp.exp(part_m - m)
    losses = m + jnp.log(total) - positive
    loss_ref[...] = jnp.broadcast_to(jnp.sum(losses, axis=0, keepdims=True), loss_ref.shape)
    target = jnp.where(diagonal, 1.0, 0.0)
    grad_full = (jnp.exp(inner - m) / total - target) * scale
    grad_in = grad_full.astype(jnp.bfloat16)
    by_own = jnp.exp(m_own - m) * (scale / total)
    by_before = (
        jnp.exp(jnp.maximum(m_before, m_far) - m) * (scale / total),
        jnp.exp(m_before - m) * (scale / total),
    )
    by_after = (
        jnp.exp(m_after - m) * (scale / total),
        jnp.exp(jnp.maximum(m_after, m_far) - m) * (scale / total),
    )
    for n in range(width // 512):
        part = pl.ds(n * 512, 512)
        side = n * 512 // half
        value = jnp.dot(grad_in, p_buf[:, part], preferred_element_type=jnp.float32)
        value = value + own_mixed[:, part] * by_own
        value = value + arriving[0, :, part].astype(jnp.float32) * by_before[side]
        value = value + arriving[1, :, part].astype(jnp.float32) * by_after[side]
        grad_ref[pl.ds(0, rows), part] = value.astype(jnp.bfloat16)
    turned = grad_full.T.astype(jnp.bfloat16)
    for n in range(width // 512):
        part = pl.ds(n * 512, 512)
        value = jnp.dot(turned, q_buf[q, :, part], preferred_element_type=jnp.float32)
        grad_ref[pl.ds(rows, rows), part] = value.astype(jnp.bfloat16)
    for copy in started:
        copy.wait_send()


def embedding_gradients(scale, all_q, blocks, emb_p, lists):
    rows, width = emb_p.shape
    count, block_rows = blocks.shape[0] * blocks.shape[1], blocks.shape[2]
    blocks = blocks.reshape(count, block_rows, width)
    places = lists.shape[1]
    anywhere = pl.BlockSpec(memory_space=pltpu.HBM)
    vmem = pl.BlockSpec(memory_space=pltpu.VMEM)
    bf16, f32 = jnp.bfloat16, jnp.float32
    return pl.pallas_call(
        lambda *refs: partial_kernel(scale, *refs),
        out_shape=(
            jax.ShapeDtypeStruct((2 * rows, width), bf16),
            jax.ShapeDtypeStruct((8, 128), f32),
        ),
        in_specs=[anywhere] * 3 + [pl.BlockSpec(memory_space=pltpu.SMEM), vmem],
        out_specs=(vmem, vmem),
        scratch_shapes=[
            pltpu.VMEM(all_q.shape, bf16),
            pltpu.VMEM(blocks.shape, bf16),
            pltpu.VMEM((rows, width), bf16),
            pltpu.VMEM((places * block_rows, width), bf16),
            pltpu.VMEM((rows, places * block_rows), bf16),
            pltpu.VMEM((rows, places * block_rows), f32),
            pltpu.VMEM((rows, width), f32),
            pltpu.VMEM((rows, width), f32),
            pltpu.VMEM((2, rows, width // 2), bf16),
            pltpu.VMEM((2, rows, width), bf16),
            pltpu.VMEM((2, rows, width // 2), bf16),
            pltpu.VMEM((2, rows, width), bf16),
            pltpu.VMEM((8, 128), f32),
            pltpu.VMEM((2, 8, 128), f32),
            pltpu.VMEM((2, 8, 128), f32),
            pltpu.VMEM((2, 8, 128), f32),
            pltpu.VMEM((8, 128), f32),
            pltpu.SemaphoreType.DMA((3,)),
            pltpu.SemaphoreType.DMA((9,)),
            pltpu.SemaphoreType.DMA((9,)),
        ],
        compiler_params=pltpu.CompilerParams(
            collective_id=1, has_side_effects=True, vmem_limit_bytes=60 * 1024 * 1024
        ),
        name="embedding_gradients",
    )(all_q, blocks, emb_p, lists, lists)


def body(queries, passages, weight, bank, neg_ids, block_home):
    count_q = queries.shape[0]
    slice_width = weight.shape[1]
    logit_scale = 1.0 / (SOFTMAX_TEMPER * math.sqrt(slice_width))
    n_dp = lax.axis_size("dp")
    n_fsdp = lax.axis_size("fsdp")
    per_dev = bank.shape[0]
    named = neg_ids.shape[1]
    core = lax.rem(lax.axis_index("fsdp"), 2)
    slots = block_home[neg_ids[0]]
    owner = slots // per_dev // n_fsdp
    local = slots % per_dev
    at_z, at_y = owner // RING, owner % RING
    on_ring = jnp.where(core == 0, at_z, at_y)
    on_row = jnp.where(core == 0, at_y, at_z)
    order = jnp.arange(named)
    earlier = (on_row[None, :] == on_row[:, None]) & (order[None, :] < order[:, None])
    rank = jnp.sum(earlier.astype(jnp.int32), axis=1)
    hit = (on_row[:, None, None] == jnp.arange(RING)[None, :, None]) & (
        rank[:, None, None] == jnp.arange(per_dev)[None, None, :]
    )
    block = on_ring * per_dev + local
    lists = jnp.sum(jnp.where(hit, block[:, None, None] + 1, 0), axis=0) - 1
    lists = jnp.broadcast_to(lists[:, :, None], lists.shape + (128,))

    blocks, all_q, emb_p, full_weight, turned, all_lists = gather_and_embed(queries, passages, weight, bank, lists)
    grad_rows, loss_local = embedding_gradients(logit_scale, all_q, blocks, emb_p, all_lists)
    grad_weight, losses, back_q, back_p = reduce_gradient(turned, grad_rows, full_weight, loss_local)
    loss = losses[0, 0] / (count_q * n_dp * n_fsdp)
    return (loss, grad_weight, back_q, back_p)


def solution(mesh):
    return jax.shard_map(
        body,
        mesh=mesh,
        in_specs=(
            P(("dp", "fsdp"), None),
            P(("dp", "fsdp"), None),
            P("fsdp", None),
            P(("dp", "fsdp"), None, None),
            P(("dp", "fsdp"), None),
            P(),
        ),
        out_specs=(P(), P(("dp", "fsdp"), None), P(("dp", "fsdp"), None), P(("dp", "fsdp"), None)),
        check_vma=False,
    )
```

```python
import math

import jax
import jax.numpy as jnp
from jax import lax
from jax.experimental import pallas as pl
from jax.experimental.pallas import tpu as pltpu
from jax.sharding import PartitionSpec as P

SOFTMAX_TEMPER = 0.25

MESH = pl.DeviceIdType.MESH
VMEM_LIMIT = 63 * 1024 * 1024
TILE = 512
RING = 4
BACK = ((0, 2), (2, 4), (4, 5), (5, 6), (6, 7), (7, 8))
ROWS = 16
PARTS = (
    (0, 768, 384, (2, 1, 0)),
    (768, 640, 384, (1, 0, 2)),
    (1408, 640, 384, (0, 2, 1)),
)


def position():
    dp = lax.axis_index("dp")
    fsdp = lax.axis_index("fsdp")
    return (lax.div(dp, RING), lax.rem(dp, RING), lax.div(fsdp, 2)), lax.rem(fsdp, 2)


def device(coords, core):
    return (coords[0] * RING + coords[1], coords[2] * 2 + core)


def shifted(coords, axis, by):
    moved = list(coords)
    moved[axis] = lax.rem(coords[axis] + by + RING, RING)
    return tuple(moved)


def greet(targets):
    barrier = pltpu.get_barrier_semaphore()
    for target in targets:
        pl.semaphore_signal(barrier, inc=1, device_id=target, device_id_type=MESH)
    pl.semaphore_wait(barrier, len(targets))


def remote(src, dst, send, recv, target):
    return pltpu.make_async_remote_copy(
        src_ref=src, dst_ref=dst, send_sem=send, recv_sem=recv, device_id=target, device_id_type=MESH
    )


def pick(rank, spot, index, columns):
    return tuple(index if i == spot else slice(None) for i in range(rank)) + (slice(None), columns)


def reduce_kernel(turned_ref, rows_ref, w_ref, loss_ref, out_ref, total_ref, backq_ref, backp_ref, *scratch):
    coords, core = position()
    sibling = device(coords, 1 - core)
    near = [[device(shifted(coords, a, by), core) for by in (1, 3)] for a in range(3)]
    far = [device(shifted(coords, a, 2), core) for a in range(3)]
    t_buf, grad_ref, w_buf, local_sem = scratch[-4:]
    scratch = scratch[:-4]
    take = [
        pltpu.make_async_copy(turned_ref, t_buf, local_sem.at[0]),
        pltpu.make_async_copy(rows_ref, grad_ref, local_sem.at[1]),
        pltpu.make_async_copy(w_ref, w_buf, local_sem.at[2]),
    ]
    for copy in take:
        copy.start()
    greet([sibling] + [d for pair in near for d in pair] + far)
    rows = backq_ref.shape[0]

    def back(lo, hi):
        @pl.loop(lo, hi)
        def _(n):
            value = lax.dot_general(
                grad_ref[...], w_buf[n], (((1,), (1,)), ((), ())), preferred_element_type=jnp.float32
            ).astype(jnp.bfloat16)
            columns = pl.ds(pl.multiple_of(n * w_buf.shape[1], 256), w_buf.shape[1])
            backq_ref[:, columns] = value[:rows]
            backp_ref[:, columns] = value[rows:]

    def share(which, i, columns):
        chunk = t_buf[which, pl.ds(pl.multiple_of(i * 256, 256), 256)]
        value = jnp.dot(chunk, grad_ref[:, columns], preferred_element_type=jnp.float32)
        return value.reshape((RING, RING, ROWS) + value.shape[1:])

    count = len(PARTS)
    paired, outgoing = scratch[:count], scratch[count : 2 * count]
    sums = [[scratch[2 * count + 3 * p + k] for k in range(3)] for p in range(count)]
    base = 5 * count
    passing = [[[scratch[base + 6 * p + 2 * k + d] for d in range(2)] for k in range(3)] for p in range(count)]
    base += 6 * count
    arriving = [[scratch[base + 3 * p + k] for k in range(3)] for p in range(count)]
    base += 3 * count
    loss_buf, send0, recv0, send, recv, loss_send, loss_recv = scratch[base:]

    started = []

    def go(copy):
        copy.start()
        started.append(copy)
        return copy

    take[0].wait()
    take[1].wait()
    first = []
    for p, (lo, width, cut, order) in enumerate(PARTS):
        columns = pl.ds(lo, width)

        @pl.loop(0, RING)
        def _(i):
            outgoing[p][i] = share(1 - core, i, columns).astype(jnp.bfloat16)

        first.append(go(remote(outgoing[p], paired[p], send0.at[p], recv0.at[p], sibling)))

    loss_buf[0, pl.ds(core, 1)] = loss_ref[...][None]
    pair_loss = go(
        remote(loss_buf.at[0, core], loss_buf.at[0, core], loss_send.at[0, 0], loss_recv.at[0, 0], sibling)
    )

    def loss_step(level, copies, slots):
        for copy in copies:
            copy.wait_recv()
        value = loss_buf[level, 0]
        for s in range(1, slots):
            value = value + loss_buf[level, s]
        return value

    def loss_send_axis(level, axis, value):
        mine = coords[axis]
        loss_buf[level, pl.ds(mine, 1)] = value[None]
        copies = []
        for n, target in enumerate((near[axis][0], near[axis][1], far[axis])):
            copies.append(
                go(
                    remote(
                        loss_buf.at[level, mine],
                        loss_buf.at[level, mine],
                        loss_send.at[level, n],
                        loss_recv.at[level, n],
                        target,
                    )
                )
            )
        return copies

    def halves(width, cut):
        return pl.ds(0, cut), pl.ds(cut, width - cut)

    def begin(p, k):
        lo, width, cut, order = PARTS[p]
        axis = order[k]
        rest = sorted(order[k:])
        spot, rank = rest.index(axis), len(rest)
        mine = coords[axis]
        both = halves(width, cut)
        source = sums[p][k]
        moves = {"far": [], "near": []}
        for d in range(2):
            moves["far"].append(
                go(
                    remote(
                        source.at[pick(rank, spot, lax.rem(mine + 2, RING), both[d])],
                        passing[p][k][d],
                        send.at[p, k, d],
                        recv.at[p, k, d],
                        near[axis][d],
                    )
                )
            )
        for d in range(2):
            by = 1 if d == 0 else 3
            moves["near"].append(
                go(
                    remote(
                        source.at[pick(rank, spot, lax.rem(mine + by, RING), both[1 - d])],
                        arriving[p][k].at[(d,) + pick(rank - 1, -1, 0, both[1 - d])],
                        send.at[p, k, 2 + d],
                        recv.at[p, k, 2 + d],
                        near[axis][d],
                    )
                )
            )
        return moves

    def relay(p, k, moves):
        lo, width, cut, order = PARTS[p]
        axis = order[k]
        rest = sorted(order[k:])
        spot, rank = rest.index(axis), len(rest)
        mine = coords[axis]
        both = halves(width, cut)
        source = sums[p][k]
        for d in range(2):
            by = 1 if d == 0 else 3
            moves["far"][d].wait_recv()
            where = pick(rank, spot, lax.rem(mine + by, RING), both[d])
            mixed = source[where].astype(jnp.float32) + passing[p][k][d][...].astype(jnp.float32)
            source[where] = mixed.astype(jnp.bfloat16)
            moves["near"].append(
                go(
                    remote(
                        source.at[where],
                        arriving[p][k].at[(d,) + pick(rank - 1, -1, 0, both[d])],
                        send.at[p, k, 4 + d],
                        recv.at[p, k, 4 + d],
                        near[axis][d],
                    )
                )
            )

    def finish(p, k, moves):
        lo, width, cut, order = PARTS[p]
        axis = order[k]
        rest = sorted(order[k:])
        spot, rank = rest.index(axis), len(rest)
        for copy in moves["near"]:
            copy.wait_recv()
        own = sums[p][k][pick(rank, spot, coords[axis], slice(None))].astype(jnp.float32)
        done = own + arriving[p][k][0].astype(jnp.float32) + arriving[p][k][1].astype(jnp.float32)
        if k < 2:
            sums[p][k + 1][...] = done.astype(jnp.bfloat16)
        else:
            out_ref[:, pl.ds(lo, width)] = done

    moves = []
    for p, (lo, width, cut, order) in enumerate(PARTS):
        columns = pl.ds(lo, width)
        first[p].wait_recv()

        @pl.loop(0, RING)
        def _(i):
            value = share(core, i, columns) + paired[p][i].astype(jnp.float32)
            sums[p][0][i] = value.astype(jnp.bfloat16)

        moves.append(begin(p, 0))

    value = loss_step(0, [pair_loss], 2)
    for k in range(3):
        loss_copies = loss_send_axis(1 + k, k, value)
        if k == 0:
            take[2].wait()
        back(*BACK[2 * k])
        for p in range(count):
            relay(p, k, moves[p])
        back(*BACK[2 * k + 1])
        for p in range(count):
            finish(p, k, moves[p])
            if k < 2:
                moves[p] = begin(p, k + 1)
        value = loss_step(1 + k, loss_copies, RING)
    total_ref[...] = value
    for copy in started:
        copy.wait_send()


def reduce_gradient(turned, grad_rows, full_weight, loss):
    width = grad_rows.shape[1]
    rows = grad_rows.shape[0] // 2
    features = full_weight.shape[0] * full_weight.shape[1]
    scratch = [pltpu.VMEM((RING,) * 3 + (ROWS, columns), jnp.bfloat16) for _, columns, _, _ in PARTS] * 2
    for _, columns, _, _ in PARTS:
        scratch += [pltpu.VMEM((RING,) * (3 - k) + (ROWS, columns), jnp.bfloat16) for k in range(3)]
    for _, columns, cut, _ in PARTS:
        for k in range(3):
            for part in (cut, columns - cut):
                scratch.append(pltpu.VMEM((RING,) * (2 - k) + (ROWS, part), jnp.bfloat16))
    for _, columns, _, _ in PARTS:
        scratch += [pltpu.VMEM((2,) + (RING,) * (2 - k) + (ROWS, columns), jnp.bfloat16) for k in range(3)]
    scratch += [
        pltpu.VMEM((4, RING, 8, 128), jnp.float32),
        pltpu.SemaphoreType.DMA((len(PARTS),)),
        pltpu.SemaphoreType.DMA((len(PARTS),)),
        pltpu.SemaphoreType.DMA((len(PARTS), 3, 6)),
        pltpu.SemaphoreType.DMA((len(PARTS), 3, 6)),
        pltpu.SemaphoreType.DMA((4, 3)),
        pltpu.SemaphoreType.DMA((4, 3)),
        pltpu.VMEM(turned.shape, jnp.bfloat16),
        pltpu.VMEM(grad_rows.shape, jnp.bfloat16),
        pltpu.VMEM(full_weight.shape, jnp.bfloat16),
        pltpu.SemaphoreType.DMA((3,)),
    ]
    hbm = pl.BlockSpec(memory_space=pltpu.HBM)
    vmem = pl.BlockSpec(memory_space=pltpu.VMEM)
    return pl.pallas_call(
        reduce_kernel,
        out_shape=(
            jax.ShapeDtypeStruct((ROWS, width), jnp.float32),
            jax.ShapeDtypeStruct((8, 128), jnp.float32),
            jax.ShapeDtypeStruct((rows, features), jnp.bfloat16),
            jax.ShapeDtypeStruct((rows, features), jnp.bfloat16),
        ),
        in_specs=[hbm, hbm, hbm, vmem],
        out_specs=(vmem,) * 4,
        scratch_shapes=scratch,
        compiler_params=pltpu.CompilerParams(
            collective_id=2, has_side_effects=True, vmem_limit_bytes=48 * 1024 * 1024
        ),
        name="reduce_gradient",
    )(turned, grad_rows, full_weight, loss)


def ring_position():
    coords, core = position()
    r = coords[0] + core * (coords[1] - coords[0])
    q = coords[1] + core * (coords[0] - coords[1])
    return r, q, coords[2], core


def ring_device(r, q, x, core):
    r = lax.rem(r + RING, RING)
    q = lax.rem(q + RING, RING)
    x = lax.rem(x + RING, RING)
    return (r * (RING - (RING - 1) * core) + q * (1 + (RING - 1) * core), x * 2 + core)


NONE = -1e30


def embed_kernel(
    scale, q_ref, p_ref, w_ref, bank_ref, list_ref,
    full_ref, turned_ref, grad_ref, loss_ref,
    w_buf, h_buf, t_buf, acc, q_buf, x_buf, p_buf, prob, score, inner,
    far_out, near_out, passing, arriving,
    far_stat, near_stat, pass_stat, arrive_stat, arrive_far,
    list_buf, index_buf, local_sem, send, recv,
):
    r, q, x, core = ring_position()
    sibling = ring_device(q, r, x, 1 - core)
    ring = [ring_device(r + by, q, x, core) for by in (1, -1)]
    row = [ring_device(r, q + by, x, core) for by in (1, -1)]
    row_far = ring_device(r, q + 2, x, core)
    line = [ring_device(r, q, x + by, core) for by in (1, -1)]
    rows, width = p_buf.shape
    depth = w_ref.shape[0]
    many = bank_ref.shape[0]
    places = list_ref.shape[1]
    half = width // 2
    own = x * 2 + core
    other = x * 2 + 1 - core

    def wrap(v):
        return lax.rem(v + RING, RING)

    local = []

    def keep(src, dst):
        copy = pltpu.make_async_copy(src, dst, local_sem.at[len(local)])
        copy.start()
        local.append(copy)
        return copy

    started = []

    def go(src, dst, target):
        n = len(started)
        copy = remote(src, dst, send.at[n], recv.at[n], target)
        copy.start()
        started.append(copy)
        return copy

    take_q = keep(q_ref, h_buf.at[pl.ds(0, rows)])
    take_p = keep(p_ref, h_buf.at[pl.ds(rows, rows)])
    take_w = keep(w_ref, w_buf.at[own])
    greet([sibling] + ring + row + [row_far] + line)

    cut_w = (pl.ds(0, depth // 2), pl.ds(depth // 2, depth // 2))
    cut_q = (pl.ds(0, rows // 2), pl.ds(rows // 2, rows // 2))

    def blocks(home, h):
        return x_buf.at[pl.ds(home * many + h * (many // 2), many // 2)]

    w_pair = go(w_ref, w_buf.at[own], sibling)
    w_near = [None, None]
    b_near = [None, None]
    for d in range(2):
        w_near[d] = [go(w_ref.at[cut_w[h]], w_buf.at[own, cut_w[h]], line[d]) for h in (d, 1 - d)]
    for d in range(2):
        b_near[d] = [
            go(bank_ref.at[pl.ds(h * (many // 2), many // 2)], blocks(r, h), ring[d]) for h in (d, 1 - d)
        ]
    list_copies = [
        go(list_ref.at[wrap(q + by)], list_buf.at[q], target) for by, target in ((1, row[0]), (-1, row[1]), (2, row_far))
    ]
    list_buf[pl.ds(q, 1)] = list_ref[pl.ds(q, 1)]
    take_b = keep(bank_ref, x_buf.at[pl.ds(r * many, many)])

    def multiply(part, first=False):
        @pl.loop(0, width // 512)
        def _(n):
            columns = pl.ds(pl.multiple_of(n * 512, 512), 512)
            term = jnp.dot(
                h_buf[:, pl.ds(pl.multiple_of(part * depth, depth), depth)],
                w_buf[part, :, columns],
                preferred_element_type=jnp.float32,
            ).reshape(2, rows, 512)
            if first:
                acc[:, :, columns] = term
            else:
                acc[:, :, columns] += term

    take_q.wait()
    take_p.wait()
    take_w.wait()
    multiply(own, True)
    w_pair.wait_recv()
    multiply(other)

    @pl.loop(0, h_buf.shape[1] // 256)
    def _(n):
        tile = h_buf[:, pl.ds(pl.multiple_of(n * 256, 256), 256)].T
        for i in range(256 // ROWS):
            place = pl.ds(pl.multiple_of(n * 128 + i // 2 * ROWS, ROWS), ROWS)
            t_buf[i % 2, place] = tile[i * ROWS : (i + 1) * ROWS]

    keep_t = keep(t_buf, turned_ref)

    across = []
    w_far = [None, None]
    w_sent = []
    for n in range(2):
        for d in range(2):
            h = d if n == 0 else 1 - d
            came = wrap(x - 1 + 2 * d) * 2 + core
            w_near[d][n].wait_recv()
            if n == 0:
                w_far[d] = go(w_buf.at[came, cut_w[h]], w_buf.at[came, cut_w[h]], line[d])
            across.append(go(w_buf.at[came, cut_w[h]], w_buf.at[came, cut_w[h]], sibling))
    w_sent += w_far + across
    multiply(wrap(x - 1) * 2 + core)
    multiply(wrap(x + 1) * 2 + core)
    b_far = [None, None]
    for d in range(2):
        came = wrap(r - 1 + 2 * d)
        b_near[d][0].wait_recv()
        b_far[d] = go(blocks(came, d), blocks(came, d), ring[d])
    for copy in across:
        copy.wait_recv()
    multiply(wrap(x - 1) * 2 + 1 - core)
    multiply(wrap(x + 1) * 2 + 1 - core)
    across = []
    last = wrap(x + 2) * 2
    for d in range(2):
        w_far[d].wait_recv()
        across.append(go(w_buf.at[last + core, cut_w[d]], w_buf.at[last + core, cut_w[d]], sibling))
    w_sent += across
    multiply(last + core)
    for copy in across:
        copy.wait_recv()
    multiply(last + 1 - core)

    q_buf[pl.ds(q, 1)] = acc[pl.ds(0, 1)].astype(jnp.bfloat16)
    q_near = [None, None]
    for d in range(2):
        q_near[d] = [go(q_buf.at[q, cut_q[h]], q_buf.at[q, cut_q[h]], row[d]) for h in (d, 1 - d)]
    p_buf[...] = acc[1].astype(jnp.bfloat16)
    keep_w = keep(w_buf, full_ref)
    for copy in list_copies:
        copy.wait_recv()
    take_index = keep(list_buf, index_buf)
    inner[...] = scale * lax.dot_general(
        q_buf[q], p_buf[...], (((1,), (1,)), ((), ())), preferred_element_type=jnp.float32
    )
    take_index.wait()
    keep_w.wait()
    for copy in w_sent:
        copy.wait_send()
    q_far = [None, None]
    for d in range(2):
        came = wrap(q - 1 + 2 * d)
        q_near[d][0].wait_recv()
        q_far[d] = go(q_buf.at[came, cut_q[d]], q_buf.at[came, cut_q[d]], row[d])
    take_b.wait()
    for d in range(2):
        b_near[d][1].wait_recv()
        b_far[d].wait_recv()

    eye = lax.broadcasted_iota(jnp.int32, (128, 128), 0) == lax.broadcasted_iota(jnp.int32, (128, 128), 1)

    def pack(stat, m, l):
        for i in range(rows // 128):
            for n, value in ((0, m), (rows // 128, l)):
                part = jnp.where(eye, value[i * 128 : (i + 1) * 128], 0.0)
                stat[pl.ds(n + i, 1)] = jnp.sum(part, axis=0, keepdims=True)

    def unpack(stat, n):
        parts = []
        for i in range(rows // 128):
            one = stat[pl.ds(n * (rows // 128) + i, 1)]
            parts.append(jnp.sum(jnp.where(eye, one, 0.0), axis=1, keepdims=True))
        return jnp.concatenate(parts, axis=0)

    def group(g):
        @pl.loop(0, places // 2)
        def _(n):
            for k in range(2):
                block = jnp.maximum(index_buf[g, 2 * n + k, 0], 0)
                w_buf[n, k * 128 : (k + 1) * 128] = x_buf[block]
            part = pl.ds(pl.multiple_of(n * 256, 256), 256)
            score[:, part] = scale * lax.dot_general(
                q_buf[g], w_buf[n], (((1,), (1,)), ((), ())), preferred_element_type=jnp.float32
            )

        top = jnp.full((rows, 128), NONE, jnp.float32)
        for k in range(places):
            valid = list_buf[g, pl.ds(k, 1)] >= 0
            top = jnp.maximum(top, jnp.where(valid, score[:, k * 128 : (k + 1) * 128], NONE))
        m = jnp.max(top, axis=1, keepdims=True)
        total = jnp.zeros((rows, 128), jnp.float32)
        for k in range(places):
            valid = list_buf[g, pl.ds(k, 1)] >= 0
            e = jnp.where(valid, jnp.exp(score[:, k * 128 : (k + 1) * 128] - m), 0.0)
            total = total + e
            prob[:, k * 128 : (k + 1) * 128] = e.astype(jnp.bfloat16)
        return m, jnp.sum(total, axis=1, keepdims=True)

    def weighted(n):
        named = w_buf[pl.ds(0, places // 2), :, pl.ds(n * TILE, TILE)]
        return jnp.dot(prob[...], named.reshape(places * 128, TILE), preferred_element_type=jnp.float32)

    tiles = half // TILE
    m_near = [None, None]
    stats = []
    plain = [None, None]

    def near_group(d):
        q_near[1 - d][1].wait_recv()
        m_near[d], l = group(wrap(q + 1 - 2 * d))
        pack(near_stat.at[d], m_near[d], l)
        stats.append(go(near_stat.at[d], arrive_stat.at[d], row[d]))
        for t in range(tiles):
            near_out[d, 1 - d, t] = weighted((1 - d) * tiles + t).astype(jnp.bfloat16)
        plain[d] = go(near_out.at[d, 1 - d], arriving.at[d, 1 - d], row[d])
        for t in range(tiles):
            n = d * tiles + t
            acc[1, :, n * TILE : (n + 1) * TILE] = weighted(n)

    m_own, l_own = group(q)
    for n in range(2 * tiles):
        acc[0, :, n * TILE : (n + 1) * TILE] = weighted(n)
    near_group(0)

    for copy in q_far:
        copy.wait_recv()
    m, l = group(wrap(q + 2))
    pack(far_stat, m, l)
    far_stats = [go(far_stat, pass_stat.at[d], row[d]) for d in range(2)]
    far = [[], []]
    for t in range(tiles):
        for d in range(2):
            far_out[d, t] = weighted(d * tiles + t).astype(jnp.bfloat16)
            far[d].append(go(far_out.at[d, t], passing.at[d, t], row[d]))
    near_group(1)

    m_in = jnp.max(inner[...], axis=1, keepdims=True)
    l_in = jnp.sum(jnp.exp(inner[...] - m_in), axis=1, keepdims=True)
    diagonal = lax.broadcasted_iota(jnp.int32, inner.shape, 0) == lax.broadcasted_iota(jnp.int32, inner.shape, 1)
    positive = jnp.sum(jnp.where(diagonal, inner[...], 0.0), axis=1, keepdims=True)

    by_near, by_far = [], []
    for d in range(2):
        far_stats[d].wait_recv()
        if d == 0:
            stats.append(go(pass_stat.at[0], arrive_far, row[0]))
        m_far = unpack(pass_stat.at[d], 0)
        both = jnp.maximum(m_near[d], m_far)
        by_near.append(jnp.exp(m_near[d] - both))
        by_far.append(jnp.exp(m_far - both))
    joined = [[], []]
    for t in range(tiles):
        for d in range(2):
            n = d * tiles + t
            far[d][t].wait_recv()
            value = acc[1, :, n * TILE : (n + 1) * TILE] * by_near[d] + passing[d, t].astype(jnp.float32) * by_far[d]
            near_out[d, d, t] = value.astype(jnp.bfloat16)
            joined[d].append(go(near_out.at[d, d, t], arriving.at[d, d, t], row[d]))

    for copy in stats:
        copy.wait_recv()
    m_before, l_before = unpack(arrive_stat.at[0], 0), unpack(arrive_stat.at[0], 1)
    m_after, l_after = unpack(arrive_stat.at[1], 0), unpack(arrive_stat.at[1], 1)
    m_far, l_far = unpack(arrive_far, 0), unpack(arrive_far, 1)
    m = m_in
    for value in (m_own, m_before, m_after, m_far):
        m = jnp.maximum(m, value)
    total = l_in * jnp.exp(m_in - m)
    for part_m, part_l in ((m_own, l_own), (m_before, l_before), (m_after, l_after), (m_far, l_far)):
        total = total + part_l * jnp.exp(part_m - m)
    losses = m + jnp.log(total) - positive
    loss_ref[...] = jnp.broadcast_to(jnp.sum(losses, axis=0, keepdims=True), loss_ref.shape)
    target = jnp.where(diagonal, 1.0, 0.0)
    grad_full = (jnp.exp(inner[...] - m) / total - target) * scale
    grad_in = grad_full.astype(jnp.bfloat16)
    turned = grad_full.T.astype(jnp.bfloat16)
    for n in range(width // 512):
        part = pl.ds(n * 512, 512)
        value = jnp.dot(turned, q_buf[q, :, part], preferred_element_type=jnp.float32)
        h_buf[pl.ds(rows, rows), part] = value.astype(jnp.bfloat16)
    keep(h_buf.at[pl.ds(rows, rows)], grad_ref.at[pl.ds(rows, rows)])
    by_own = jnp.exp(m_own - m) * (scale / total)
    by_before = (
        jnp.exp(jnp.maximum(m_before, m_far) - m) * (scale / total),
        jnp.exp(m_before - m) * (scale / total),
    )
    by_after = (
        jnp.exp(m_after - m) * (scale / total),
        jnp.exp(jnp.maximum(m_after, m_far) - m) * (scale / total),
    )
    for copy in plain:
        copy.wait_recv()
    for t in range(tiles):
        for side in range(2):
            joined[side][t].wait_recv()
            part = pl.ds((side * tiles + t) * TILE, TILE)
            value = jnp.dot(grad_in, p_buf[:, part], preferred_element_type=jnp.float32)
            value = value + acc[0, :, part] * by_own
            value = value + arriving[0, side, t].astype(jnp.float32) * by_before[side]
            value = value + arriving[1, side, t].astype(jnp.float32) * by_after[side]
            h_buf[pl.ds(0, rows), part] = value.astype(jnp.bfloat16)
    keep(h_buf.at[pl.ds(0, rows)], grad_ref.at[pl.ds(0, rows)])
    for copy in local:
        if not any(copy is c for c in (take_q, take_p, take_w, take_b, take_index, keep_w)):
            copy.wait()
    for copy in started:
        if not any(copy is c for c in w_sent):
            copy.wait_send()


def embedding_gradients(scale, queries, passages, weight, bank, lists):
    rows, features = queries.shape
    depth, width = weight.shape
    parts = features // depth
    many, block_rows = bank.shape[:2]
    places = lists.shape[1]
    half = width // 2
    bf16, f32 = jnp.bfloat16, jnp.float32
    hbm = pl.BlockSpec(memory_space=pltpu.HBM)
    vmem = pl.BlockSpec(memory_space=pltpu.VMEM)
    return pl.pallas_call(
        lambda *refs: embed_kernel(scale, *refs),
        out_shape=(
            jax.ShapeDtypeStruct((parts, depth, width), bf16),
            jax.ShapeDtypeStruct((2, features // 2, 2 * rows), bf16),
            jax.ShapeDtypeStruct((2 * rows, width), bf16),
            jax.ShapeDtypeStruct((8, 128), f32),
        ),
        in_specs=[hbm] * 4 + [vmem],
        out_specs=(hbm, hbm, hbm, vmem),
        scratch_shapes=[
            pltpu.VMEM((parts, depth, width), bf16),
            pltpu.VMEM((2 * rows, features), bf16),
            pltpu.VMEM((2, features // 2, 2 * rows), bf16),
            pltpu.VMEM((2, rows, width), f32),
            pltpu.VMEM((RING, rows, width), bf16),
            pltpu.VMEM((RING * many, block_rows, width), bf16),
            pltpu.VMEM((rows, width), bf16),
            pltpu.VMEM((rows, places * block_rows), bf16),
            pltpu.VMEM((rows, places * block_rows), f32),
            pltpu.VMEM((rows, rows), f32),
            pltpu.VMEM((2, half // TILE, rows, TILE), bf16),
            pltpu.VMEM((2, 2, half // TILE, rows, TILE), bf16),
            pltpu.VMEM((2, half // TILE, rows, TILE), bf16),
            pltpu.VMEM((2, 2, half // TILE, rows, TILE), bf16),
            pltpu.VMEM((8, 128), f32),
            pltpu.VMEM((2, 8, 128), f32),
            pltpu.VMEM((2, 8, 128), f32),
            pltpu.VMEM((2, 8, 128), f32),
            pltpu.VMEM((8, 128), f32),
            pltpu.VMEM(lists.shape, jnp.int32),
            pltpu.SMEM(lists.shape, jnp.int32),
            pltpu.SemaphoreType.DMA((9,)),
            pltpu.SemaphoreType.DMA((43,)),
            pltpu.SemaphoreType.DMA((43,)),
        ],
        compiler_params=pltpu.CompilerParams(
            collective_id=0, has_side_effects=True, vmem_limit_bytes=VMEM_LIMIT
        ),
        name="embedding_gradients",
    )(queries, passages, weight, bank, lists)


def body(queries, passages, weight, bank, neg_ids, block_home):
    count_q = queries.shape[0]
    slice_width = weight.shape[1]
    logit_scale = 1.0 / (SOFTMAX_TEMPER * math.sqrt(slice_width))
    n_dp = lax.axis_size("dp")
    n_fsdp = lax.axis_size("fsdp")
    per_dev = bank.shape[0]
    named = neg_ids.shape[1]
    core = lax.rem(lax.axis_index("fsdp"), 2)
    slots = block_home[neg_ids[0]]
    owner = slots // per_dev // n_fsdp
    local = slots % per_dev
    at_z, at_y = owner // RING, owner % RING
    on_ring = jnp.where(core == 0, at_z, at_y)
    on_row = jnp.where(core == 0, at_y, at_z)
    order = jnp.arange(named)
    earlier = (on_row[None, :] == on_row[:, None]) & (order[None, :] < order[:, None])
    rank = jnp.sum(earlier.astype(jnp.int32), axis=1)
    hit = (on_row[:, None, None] == jnp.arange(RING)[None, :, None]) & (
        rank[:, None, None] == jnp.arange(per_dev)[None, None, :]
    )
    block = on_ring * per_dev + local
    lists = jnp.sum(jnp.where(hit, block[:, None, None] + 1, 0), axis=0) - 1
    lists = jnp.broadcast_to(lists[:, :, None], lists.shape + (128,))

    full_weight, turned, grad_rows, loss_local = embedding_gradients(
        logit_scale, queries, passages, weight, bank, lists
    )
    grad_weight, losses, back_q, back_p = reduce_gradient(turned, grad_rows, full_weight, loss_local)
    loss = losses[0, 0] / (count_q * n_dp * n_fsdp)
    return (loss, grad_weight, back_q, back_p)


def solution(mesh):
    return jax.shard_map(
        body,
        mesh=mesh,
        in_specs=(
            P(("dp", "fsdp"), None),
            P(("dp", "fsdp"), None),
            P("fsdp", None),
            P(("dp", "fsdp"), None, None),
            P(("dp", "fsdp"), None),
            P(),
        ),
        out_specs=(P(), P(("dp", "fsdp"), None), P(("dp", "fsdp"), None), P(("dp", "fsdp"), None)),
        check_vma=False,
    )
```

```python
import math

import jax
import jax.numpy as jnp
from jax import lax
from jax.experimental import pallas as pl
from jax.experimental.pallas import tpu as pltpu
from jax.sharding import PartitionSpec as P

SOFTMAX_TEMPER = 0.25

MESH = pl.DeviceIdType.MESH
VMEM_LIMIT = 63 * 1024 * 1024
TILE = 512
RING = 4
BACK = ((0, 2), (2, 4), (4, 5), (5, 6), (6, 7), (7, 8))
ROWS = 16
PARTS = (
    (0, 768, 384, (2, 1, 0)),
    (768, 640, 384, (1, 0, 2)),
    (1408, 640, 384, (0, 2, 1)),
)


def position():
    dp = lax.axis_index("dp")
    fsdp = lax.axis_index("fsdp")
    return (lax.div(dp, RING), lax.rem(dp, RING), lax.div(fsdp, 2)), lax.rem(fsdp, 2)


def device(coords, core):
    return (coords[0] * RING + coords[1], coords[2] * 2 + core)


def shifted(coords, axis, by):
    moved = list(coords)
    moved[axis] = lax.rem(coords[axis] + by + RING, RING)
    return tuple(moved)


def greet(targets):
    barrier = pltpu.get_barrier_semaphore()
    for target in targets:
        pl.semaphore_signal(barrier, inc=1, device_id=target, device_id_type=MESH)
    pl.semaphore_wait(barrier, len(targets))


def remote(src, dst, send, recv, target):
    return pltpu.make_async_remote_copy(
        src_ref=src, dst_ref=dst, send_sem=send, recv_sem=recv, device_id=target, device_id_type=MESH
    )


def pick(rank, spot, index, columns):
    return tuple(index if i == spot else slice(None) for i in range(rank)) + (slice(None), columns)


def reduce_kernel(turned_ref, rows_ref, w_ref, loss_ref, out_ref, total_ref, backq_ref, backp_ref, *scratch):
    coords, core = position()
    sibling = device(coords, 1 - core)
    near = [[device(shifted(coords, a, by), core) for by in (1, 3)] for a in range(3)]
    far = [device(shifted(coords, a, 2), core) for a in range(3)]
    t_buf, grad_ref, w_buf, local_sem = scratch[-4:]
    scratch = scratch[:-4]
    take = [
        pltpu.make_async_copy(turned_ref, t_buf, local_sem.at[0]),
        pltpu.make_async_copy(rows_ref, grad_ref, local_sem.at[1]),
        pltpu.make_async_copy(w_ref, w_buf, local_sem.at[2]),
    ]
    for copy in take:
        copy.start()
    greet([sibling] + [d for pair in near for d in pair] + far)
    rows = backq_ref.shape[0]

    def back(lo, hi):
        @pl.loop(lo, hi)
        def _(n):
            value = lax.dot_general(
                grad_ref[...], w_buf[n], (((1,), (1,)), ((), ())), preferred_element_type=jnp.float32
            ).astype(jnp.bfloat16)
            columns = pl.ds(pl.multiple_of(n * w_buf.shape[1], 256), w_buf.shape[1])
            backq_ref[:, columns] = value[:rows]
            backp_ref[:, columns] = value[rows:]

    def share(which, i, columns):
        chunk = t_buf[which, pl.ds(pl.multiple_of(i * 256, 256), 256)]
        value = jnp.dot(chunk, grad_ref[:, columns], preferred_element_type=jnp.float32)
        return value.reshape((RING, RING, ROWS) + value.shape[1:])

    count = len(PARTS)
    paired, outgoing = scratch[:count], scratch[count : 2 * count]
    sums = [[scratch[2 * count + 3 * p + k] for k in range(3)] for p in range(count)]
    base = 5 * count
    passing = [[[scratch[base + 6 * p + 2 * k + d] for d in range(2)] for k in range(3)] for p in range(count)]
    base += 6 * count
    arriving = [[scratch[base + 3 * p + k] for k in range(3)] for p in range(count)]
    base += 3 * count
    loss_buf, send0, recv0, send, recv, loss_send, loss_recv = scratch[base:]

    started = []

    def go(copy):
        copy.start()
        started.append(copy)
        return copy

    take[0].wait()
    take[1].wait()
    first = []
    for p, (lo, width, cut, order) in enumerate(PARTS):
        columns = pl.ds(lo, width)

        @pl.loop(0, RING)
        def _(i):
            outgoing[p][i] = share(1 - core, i, columns).astype(jnp.bfloat16)

        first.append(go(remote(outgoing[p], paired[p], send0.at[p], recv0.at[p], sibling)))

    loss_buf[0, pl.ds(core, 1)] = loss_ref[...][None]
    pair_loss = go(
        remote(loss_buf.at[0, core], loss_buf.at[0, core], loss_send.at[0, 0], loss_recv.at[0, 0], sibling)
    )

    def loss_step(level, copies, slots):
        for copy in copies:
            copy.wait_recv()
        value = loss_buf[level, 0]
        for s in range(1, slots):
            value = value + loss_buf[level, s]
        return value

    def loss_send_axis(level, axis, value):
        mine = coords[axis]
        loss_buf[level, pl.ds(mine, 1)] = value[None]
        copies = []
        for n, target in enumerate((near[axis][0], near[axis][1], far[axis])):
            copies.append(
                go(
                    remote(
                        loss_buf.at[level, mine],
                        loss_buf.at[level, mine],
                        loss_send.at[level, n],
                        loss_recv.at[level, n],
                        target,
                    )
                )
            )
        return copies

    def halves(width, cut):
        return pl.ds(0, cut), pl.ds(cut, width - cut)

    def begin(p, k):
        lo, width, cut, order = PARTS[p]
        axis = order[k]
        rest = sorted(order[k:])
        spot, rank = rest.index(axis), len(rest)
        mine = coords[axis]
        both = halves(width, cut)
        source = sums[p][k]
        moves = {"far": [], "near": []}
        for d in range(2):
            moves["far"].append(
                go(
                    remote(
                        source.at[pick(rank, spot, lax.rem(mine + 2, RING), both[d])],
                        passing[p][k][d],
                        send.at[p, k, d],
                        recv.at[p, k, d],
                        near[axis][d],
                    )
                )
            )
        for d in range(2):
            by = 1 if d == 0 else 3
            moves["near"].append(
                go(
                    remote(
                        source.at[pick(rank, spot, lax.rem(mine + by, RING), both[1 - d])],
                        arriving[p][k].at[(d,) + pick(rank - 1, -1, 0, both[1 - d])],
                        send.at[p, k, 2 + d],
                        recv.at[p, k, 2 + d],
                        near[axis][d],
                    )
                )
            )
        return moves

    def relay(p, k, moves):
        lo, width, cut, order = PARTS[p]
        axis = order[k]
        rest = sorted(order[k:])
        spot, rank = rest.index(axis), len(rest)
        mine = coords[axis]
        both = halves(width, cut)
        source = sums[p][k]
        for d in range(2):
            by = 1 if d == 0 else 3
            moves["far"][d].wait_recv()
            where = pick(rank, spot, lax.rem(mine + by, RING), both[d])
            mixed = source[where].astype(jnp.float32) + passing[p][k][d][...].astype(jnp.float32)
            source[where] = mixed.astype(jnp.bfloat16)
            moves["near"].append(
                go(
                    remote(
                        source.at[where],
                        arriving[p][k].at[(d,) + pick(rank - 1, -1, 0, both[d])],
                        send.at[p, k, 4 + d],
                        recv.at[p, k, 4 + d],
                        near[axis][d],
                    )
                )
            )

    def finish(p, k, moves):
        lo, width, cut, order = PARTS[p]
        axis = order[k]
        rest = sorted(order[k:])
        spot, rank = rest.index(axis), len(rest)
        for copy in moves["near"]:
            copy.wait_recv()
        own = sums[p][k][pick(rank, spot, coords[axis], slice(None))].astype(jnp.float32)
        done = own + arriving[p][k][0].astype(jnp.float32) + arriving[p][k][1].astype(jnp.float32)
        if k < 2:
            sums[p][k + 1][...] = done.astype(jnp.bfloat16)
        else:
            out_ref[:, pl.ds(lo, width)] = done

    moves = []
    for p, (lo, width, cut, order) in enumerate(PARTS):
        columns = pl.ds(lo, width)
        first[p].wait_recv()

        @pl.loop(0, RING)
        def _(i):
            value = share(core, i, columns) + paired[p][i].astype(jnp.float32)
            sums[p][0][i] = value.astype(jnp.bfloat16)

        moves.append(begin(p, 0))

    value = loss_step(0, [pair_loss], 2)
    for k in range(3):
        loss_copies = loss_send_axis(1 + k, k, value)
        if k == 0:
            take[2].wait()
        back(*BACK[2 * k])
        for p in range(count):
            relay(p, k, moves[p])
        back(*BACK[2 * k + 1])
        for p in range(count):
            finish(p, k, moves[p])
            if k < 2:
                moves[p] = begin(p, k + 1)
        value = loss_step(1 + k, loss_copies, RING)
    total_ref[...] = value
    for copy in started:
        copy.wait_send()


def reduce_gradient(turned, grad_rows, full_weight, loss):
    width = grad_rows.shape[1]
    rows = grad_rows.shape[0] // 2
    features = full_weight.shape[0] * full_weight.shape[1]
    scratch = [pltpu.VMEM((RING,) * 3 + (ROWS, columns), jnp.bfloat16) for _, columns, _, _ in PARTS] * 2
    for _, columns, _, _ in PARTS:
        scratch += [pltpu.VMEM((RING,) * (3 - k) + (ROWS, columns), jnp.bfloat16) for k in range(3)]
    for _, columns, cut, _ in PARTS:
        for k in range(3):
            for part in (cut, columns - cut):
                scratch.append(pltpu.VMEM((RING,) * (2 - k) + (ROWS, part), jnp.bfloat16))
    for _, columns, _, _ in PARTS:
        scratch += [pltpu.VMEM((2,) + (RING,) * (2 - k) + (ROWS, columns), jnp.bfloat16) for k in range(3)]
    scratch += [
        pltpu.VMEM((4, RING, 8, 128), jnp.float32),
        pltpu.SemaphoreType.DMA((len(PARTS),)),
        pltpu.SemaphoreType.DMA((len(PARTS),)),
        pltpu.SemaphoreType.DMA((len(PARTS), 3, 6)),
        pltpu.SemaphoreType.DMA((len(PARTS), 3, 6)),
        pltpu.SemaphoreType.DMA((4, 3)),
        pltpu.SemaphoreType.DMA((4, 3)),
        pltpu.VMEM(turned.shape, jnp.bfloat16),
        pltpu.VMEM(grad_rows.shape, jnp.bfloat16),
        pltpu.VMEM(full_weight.shape, jnp.bfloat16),
        pltpu.SemaphoreType.DMA((3,)),
    ]
    hbm = pl.BlockSpec(memory_space=pltpu.HBM)
    vmem = pl.BlockSpec(memory_space=pltpu.VMEM)
    return pl.pallas_call(
        reduce_kernel,
        out_shape=(
            jax.ShapeDtypeStruct((ROWS, width), jnp.float32),
            jax.ShapeDtypeStruct((8, 128), jnp.float32),
            jax.ShapeDtypeStruct((rows, features), jnp.bfloat16),
            jax.ShapeDtypeStruct((rows, features), jnp.bfloat16),
        ),
        in_specs=[hbm, hbm, hbm, vmem],
        out_specs=(vmem,) * 4,
        scratch_shapes=scratch,
        compiler_params=pltpu.CompilerParams(
            collective_id=2, has_side_effects=True, vmem_limit_bytes=48 * 1024 * 1024
        ),
        name="reduce_gradient",
    )(turned, grad_rows, full_weight, loss)


def ring_position():
    coords, core = position()
    r = coords[0] + core * (coords[1] - coords[0])
    q = coords[1] + core * (coords[0] - coords[1])
    return r, q, coords[2], core


def ring_device(r, q, x, core):
    r = lax.rem(r + RING, RING)
    q = lax.rem(q + RING, RING)
    x = lax.rem(x + RING, RING)
    return (r * (RING - (RING - 1) * core) + q * (1 + (RING - 1) * core), x * 2 + core)


NONE = -1e30


def embed_kernel(
    scale, q_ref, p_ref, w_ref, bank_ref, list_ref,
    full_ref, turned_ref, grad_ref, loss_ref,
    w_buf, h_buf, t_buf, acc, q_buf, x_buf, p_buf, prob, score, inner,
    far_out, near_out, passing, arriving,
    far_stat, near_stat, pass_stat, arrive_stat, arrive_far,
    list_buf, index_buf, local_sem, send, recv,
):
    r, q, x, core = ring_position()
    sibling = ring_device(q, r, x, 1 - core)
    ring = [ring_device(r + by, q, x, core) for by in (1, -1)]
    row = [ring_device(r, q + by, x, core) for by in (1, -1)]
    row_far = ring_device(r, q + 2, x, core)
    line = [ring_device(r, q, x + by, core) for by in (1, -1)]
    rows, width = p_buf.shape
    depth = w_ref.shape[0]
    many = bank_ref.shape[0]
    places = list_ref.shape[1]
    half = width // 2
    own = x * 2 + core
    other = x * 2 + 1 - core

    def wrap(v):
        return lax.rem(v + RING, RING)

    local = []

    def keep(src, dst):
        copy = pltpu.make_async_copy(src, dst, local_sem.at[len(local)])
        copy.start()
        local.append(copy)
        return copy

    started = []

    def go(src, dst, target):
        n = len(started)
        copy = remote(src, dst, send.at[n], recv.at[n], target)
        copy.start()
        started.append(copy)
        return copy

    take_q = keep(q_ref, h_buf.at[pl.ds(0, rows)])
    take_p = keep(p_ref, h_buf.at[pl.ds(rows, rows)])
    take_w = keep(w_ref, w_buf.at[own])
    greet([sibling] + ring + row + [row_far] + line)

    cut_w = (pl.ds(0, depth // 2), pl.ds(depth // 2, depth // 2))
    cut_q = (pl.ds(0, rows // 2), pl.ds(rows // 2, rows // 2))

    def blocks(home, h):
        return x_buf.at[pl.ds(home * many + h * (many // 2), many // 2)]

    w_pair = go(w_ref, w_buf.at[own], sibling)
    w_near = [None, None]
    b_near = [None, None]
    for d in range(2):
        w_near[d] = [go(w_ref.at[cut_w[h]], w_buf.at[own, cut_w[h]], line[d]) for h in (d, 1 - d)]
    for d in range(2):
        b_near[d] = [
            go(bank_ref.at[pl.ds(h * (many // 2), many // 2)], blocks(r, h), ring[d]) for h in (d, 1 - d)
        ]
    list_copies = [
        go(list_ref.at[wrap(q + by)], list_buf.at[q], target) for by, target in ((1, row[0]), (-1, row[1]), (2, row_far))
    ]
    list_buf[pl.ds(q, 1)] = list_ref[pl.ds(q, 1)]
    take_b = keep(bank_ref, x_buf.at[pl.ds(r * many, many)])

    def multiply(part, first=False):
        @pl.loop(0, width // 512)
        def _(n):
            columns = pl.ds(pl.multiple_of(n * 512, 512), 512)
            term = jnp.dot(
                h_buf[:, pl.ds(pl.multiple_of(part * depth, depth), depth)],
                w_buf[part, :, columns],
                preferred_element_type=jnp.float32,
            ).reshape(2, rows, 512)
            if first:
                acc[:, :, columns] = term
            else:
                acc[:, :, columns] += term

    take_q.wait()
    take_p.wait()
    take_w.wait()
    multiply(own, True)
    w_pair.wait_recv()
    multiply(other)

    @pl.loop(0, h_buf.shape[1] // 256)
    def _(n):
        tile = h_buf[:, pl.ds(pl.multiple_of(n * 256, 256), 256)].T
        for i in range(256 // ROWS):
            place = pl.ds(pl.multiple_of(n * 128 + i // 2 * ROWS, ROWS), ROWS)
            t_buf[i % 2, place] = tile[i * ROWS : (i + 1) * ROWS]

    keep_t = keep(t_buf, turned_ref)

    across = []
    w_far = [None, None]
    w_sent = []
    for n in range(2):
        for d in range(2):
            h = d if n == 0 else 1 - d
            came = wrap(x - 1 + 2 * d) * 2 + core
            w_near[d][n].wait_recv()
            if n == 0:
                w_far[d] = go(w_buf.at[came, cut_w[h]], w_buf.at[came, cut_w[h]], line[d])
            across.append(go(w_buf.at[came, cut_w[h]], w_buf.at[came, cut_w[h]], sibling))
    w_sent += w_far + across
    multiply(wrap(x - 1) * 2 + core)
    multiply(wrap(x + 1) * 2 + core)
    b_far = [None, None]
    for d in range(2):
        came = wrap(r - 1 + 2 * d)
        b_near[d][0].wait_recv()
        b_far[d] = go(blocks(came, d), blocks(came, d), ring[d])
    for copy in across:
        copy.wait_recv()
    multiply(wrap(x - 1) * 2 + 1 - core)
    multiply(wrap(x + 1) * 2 + 1 - core)
    across = []
    last = wrap(x + 2) * 2
    for d in range(2):
        w_far[d].wait_recv()
        across.append(go(w_buf.at[last + core, cut_w[d]], w_buf.at[last + core, cut_w[d]], sibling))
    w_sent += across
    multiply(last + core)
    for copy in across:
        copy.wait_recv()
    multiply(last + 1 - core)

    q_buf[pl.ds(q, 1)] = acc[pl.ds(0, 1)].astype(jnp.bfloat16)
    p_buf[...] = acc[1].astype(jnp.bfloat16)
    keep_w = keep(w_buf, full_ref)
    for copy in list_copies:
        copy.wait_recv()
    take_index = keep(list_buf, index_buf)
    inner[...] = scale * lax.dot_general(
        q_buf[q], p_buf[...], (((1,), (1,)), ((), ())), preferred_element_type=jnp.float32
    )
    take_index.wait()
    keep_w.wait()
    for copy in w_sent:
        copy.wait_send()
    for copy in b_far:
        copy.wait_send()
    q_near = [[], []]
    for d in range(2):
        q_near[d].append(go(q_buf.at[q, cut_q[d]], q_buf.at[q, cut_q[d]], row[d]))
    take_b.wait()
    for d in range(2):
        b_near[d][1].wait_recv()
        b_far[d].wait_recv()

    eye = lax.broadcasted_iota(jnp.int32, (128, 128), 0) == lax.broadcasted_iota(jnp.int32, (128, 128), 1)

    def pack(stat, m, l):
        for i in range(rows // 128):
            for n, value in ((0, m), (rows // 128, l)):
                part = jnp.where(eye, value[i * 128 : (i + 1) * 128], 0.0)
                stat[pl.ds(n + i, 1)] = jnp.sum(part, axis=0, keepdims=True)

    def unpack(stat, n):
        parts = []
        for i in range(rows // 128):
            one = stat[pl.ds(n * (rows // 128) + i, 1)]
            parts.append(jnp.sum(jnp.where(eye, one, 0.0), axis=1, keepdims=True))
        return jnp.concatenate(parts, axis=0)

    def group(g):
        @pl.loop(0, places // 2)
        def _(n):
            for k in range(2):
                block = jnp.maximum(index_buf[g, 2 * n + k, 0], 0)
                w_buf[n, k * 128 : (k + 1) * 128] = x_buf[block]
            part = pl.ds(pl.multiple_of(n * 256, 256), 256)
            score[:, part] = scale * lax.dot_general(
                q_buf[g], w_buf[n], (((1,), (1,)), ((), ())), preferred_element_type=jnp.float32
            )

        top = jnp.full((rows, 128), NONE, jnp.float32)
        for k in range(places):
            valid = list_buf[g, pl.ds(k, 1)] >= 0
            top = jnp.maximum(top, jnp.where(valid, score[:, k * 128 : (k + 1) * 128], NONE))
        m = jnp.max(top, axis=1, keepdims=True)
        total = jnp.zeros((rows, 128), jnp.float32)
        for k in range(places):
            valid = list_buf[g, pl.ds(k, 1)] >= 0
            e = jnp.where(valid, jnp.exp(score[:, k * 128 : (k + 1) * 128] - m), 0.0)
            total = total + e
            prob[:, k * 128 : (k + 1) * 128] = e.astype(jnp.bfloat16)
        return m, jnp.sum(total, axis=1, keepdims=True)

    def weighted(n):
        named = w_buf[pl.ds(0, places // 2), :, pl.ds(n * TILE, TILE)]
        return jnp.dot(prob[...], named.reshape(places * 128, TILE), preferred_element_type=jnp.float32)

    tiles = half // TILE
    m_near = [None, None]
    stats = []
    plain = [None, None]

    def near_group(d):
        q_near[1 - d][1].wait_recv()
        m_near[d], l = group(wrap(q + 1 - 2 * d))
        pack(near_stat.at[d], m_near[d], l)
        stats.append(go(near_stat.at[d], arrive_stat.at[d], row[d]))
        for t in range(tiles):
            near_out[d, 1 - d, t] = weighted((1 - d) * tiles + t).astype(jnp.bfloat16)
        plain[d] = go(near_out.at[d, 1 - d], arriving.at[d, 1 - d], row[d])
        for t in range(tiles):
            n = d * tiles + t
            acc[1, :, n * TILE : (n + 1) * TILE] = weighted(n)

    m_own, l_own = group(q)
    for d in range(2):
        q_near[d].append(go(q_buf.at[q, cut_q[1 - d]], q_buf.at[q, cut_q[1 - d]], row[d]))
    for n in range(2 * tiles):
        acc[0, :, n * TILE : (n + 1) * TILE] = weighted(n)
    q_far = [None, None]
    for d in range(2):
        came = wrap(q - 1 + 2 * d)
        q_near[d][0].wait_recv()
        q_far[d] = go(q_buf.at[came, cut_q[d]], q_buf.at[came, cut_q[d]], row[d])
    near_group(0)
    near_group(1)

    for copy in q_far:
        copy.wait_recv()
    m, l = group(wrap(q + 2))
    pack(far_stat, m, l)
    far_stats = [go(far_stat, pass_stat.at[d], row[d]) for d in range(2)]
    far = [[], []]
    for t in range(tiles):
        for d in range(2):
            far_out[d, t] = weighted(d * tiles + t).astype(jnp.bfloat16)
            far[d].append(go(far_out.at[d, t], passing.at[d, t], row[d]))

    m_in = jnp.max(inner[...], axis=1, keepdims=True)
    l_in = jnp.sum(jnp.exp(inner[...] - m_in), axis=1, keepdims=True)
    diagonal = lax.broadcasted_iota(jnp.int32, inner.shape, 0) == lax.broadcasted_iota(jnp.int32, inner.shape, 1)
    positive = jnp.sum(jnp.where(diagonal, inner[...], 0.0), axis=1, keepdims=True)

    by_near, by_far = [], []
    for d in range(2):
        far_stats[d].wait_recv()
        if d == 0:
            stats.append(go(pass_stat.at[0], arrive_far, row[0]))
        m_far = unpack(pass_stat.at[d], 0)
        both = jnp.maximum(m_near[d], m_far)
        by_near.append(jnp.exp(m_near[d] - both))
        by_far.append(jnp.exp(m_far - both))
    joined = [[], []]
    for t in range(tiles):
        for d in range(2):
            n = d * tiles + t
            far[d][t].wait_recv()
            value = acc[1, :, n * TILE : (n + 1) * TILE] * by_near[d] + passing[d, t].astype(jnp.float32) * by_far[d]
            near_out[d, d, t] = value.astype(jnp.bfloat16)
            joined[d].append(go(near_out.at[d, d, t], arriving.at[d, d, t], row[d]))

    for copy in stats:
        copy.wait_recv()
    m_before, l_before = unpack(arrive_stat.at[0], 0), unpack(arrive_stat.at[0], 1)
    m_after, l_after = unpack(arrive_stat.at[1], 0), unpack(arrive_stat.at[1], 1)
    m_far, l_far = unpack(arrive_far, 0), unpack(arrive_far, 1)
    m = m_in
    for value in (m_own, m_before, m_after, m_far):
        m = jnp.maximum(m, value)
    total = l_in * jnp.exp(m_in - m)
    for part_m, part_l in ((m_own, l_own), (m_before, l_before), (m_after, l_after), (m_far, l_far)):
        total = total + part_l * jnp.exp(part_m - m)
    losses = m + jnp.log(total) - positive
    loss_ref[...] = jnp.broadcast_to(jnp.sum(losses, axis=0, keepdims=True), loss_ref.shape)
    target = jnp.where(diagonal, 1.0, 0.0)
    grad_full = (jnp.exp(inner[...] - m) / total - target) * scale
    grad_in = grad_full.astype(jnp.bfloat16)
    turned = grad_full.T.astype(jnp.bfloat16)
    for n in range(width // 512):
        part = pl.ds(n * 512, 512)
        value = jnp.dot(turned, q_buf[q, :, part], preferred_element_type=jnp.float32)
        h_buf[pl.ds(rows, rows), part] = value.astype(jnp.bfloat16)
    keep(h_buf.at[pl.ds(rows, rows)], grad_ref.at[pl.ds(rows, rows)])
    by_own = jnp.exp(m_own - m) * (scale / total)
    by_before = (
        jnp.exp(jnp.maximum(m_before, m_far) - m) * (scale / total),
        jnp.exp(m_before - m) * (scale / total),
    )
    by_after = (
        jnp.exp(m_after - m) * (scale / total),
        jnp.exp(jnp.maximum(m_after, m_far) - m) * (scale / total),
    )
    for copy in plain:
        copy.wait_recv()
    for t in range(tiles):
        for side in range(2):
            joined[side][t].wait_recv()
            part = pl.ds((side * tiles + t) * TILE, TILE)
            value = jnp.dot(grad_in, p_buf[:, part], preferred_element_type=jnp.float32)
            value = value + acc[0, :, part] * by_own
            value = value + arriving[0, side, t].astype(jnp.float32) * by_before[side]
            value = value + arriving[1, side, t].astype(jnp.float32) * by_after[side]
            h_buf[pl.ds(0, rows), part] = value.astype(jnp.bfloat16)
    keep(h_buf.at[pl.ds(0, rows)], grad_ref.at[pl.ds(0, rows)])
    for copy in local:
        if not any(copy is c for c in (take_q, take_p, take_w, take_b, take_index, keep_w)):
            copy.wait()
    for copy in started:
        if not any(copy is c for c in w_sent + b_far):
            copy.wait_send()


def embedding_gradients(scale, queries, passages, weight, bank, lists):
    rows, features = queries.shape
    depth, width = weight.shape
    parts = features // depth
    many, block_rows = bank.shape[:2]
    places = lists.shape[1]
    half = width // 2
    bf16, f32 = jnp.bfloat16, jnp.float32
    hbm = pl.BlockSpec(memory_space=pltpu.HBM)
    vmem = pl.BlockSpec(memory_space=pltpu.VMEM)
    return pl.pallas_call(
        lambda *refs: embed_kernel(scale, *refs),
        out_shape=(
            jax.ShapeDtypeStruct((parts, depth, width), bf16),
            jax.ShapeDtypeStruct((2, features // 2, 2 * rows), bf16),
            jax.ShapeDtypeStruct((2 * rows, width), bf16),
            jax.ShapeDtypeStruct((8, 128), f32),
        ),
        in_specs=[hbm] * 4 + [vmem],
        out_specs=(hbm, hbm, hbm, vmem),
        scratch_shapes=[
            pltpu.VMEM((parts, depth, width), bf16),
            pltpu.VMEM((2 * rows, features), bf16),
            pltpu.VMEM((2, features // 2, 2 * rows), bf16),
            pltpu.VMEM((2, rows, width), f32),
            pltpu.VMEM((RING, rows, width), bf16),
            pltpu.VMEM((RING * many, block_rows, width), bf16),
            pltpu.VMEM((rows, width), bf16),
            pltpu.VMEM((rows, places * block_rows), bf16),
            pltpu.VMEM((rows, places * block_rows), f32),
            pltpu.VMEM((rows, rows), f32),
            pltpu.VMEM((2, half // TILE, rows, TILE), bf16),
            pltpu.VMEM((2, 2, half // TILE, rows, TILE), bf16),
            pltpu.VMEM((2, half // TILE, rows, TILE), bf16),
            pltpu.VMEM((2, 2, half // TILE, rows, TILE), bf16),
            pltpu.VMEM((8, 128), f32),
            pltpu.VMEM((2, 8, 128), f32),
            pltpu.VMEM((2, 8, 128), f32),
            pltpu.VMEM((2, 8, 128), f32),
            pltpu.VMEM((8, 128), f32),
            pltpu.VMEM(lists.shape, jnp.int32),
            pltpu.SMEM(lists.shape, jnp.int32),
            pltpu.SemaphoreType.DMA((9,)),
            pltpu.SemaphoreType.DMA((43,)),
            pltpu.SemaphoreType.DMA((43,)),
        ],
        compiler_params=pltpu.CompilerParams(
            collective_id=0, has_side_effects=True, vmem_limit_bytes=VMEM_LIMIT
        ),
        name="embedding_gradients",
    )(queries, passages, weight, bank, lists)


def body(queries, passages, weight, bank, neg_ids, block_home):
    count_q = queries.shape[0]
    slice_width = weight.shape[1]
    logit_scale = 1.0 / (SOFTMAX_TEMPER * math.sqrt(slice_width))
    n_dp = lax.axis_size("dp")
    n_fsdp = lax.axis_size("fsdp")
    per_dev = bank.shape[0]
    named = neg_ids.shape[1]
    core = lax.rem(lax.axis_index("fsdp"), 2)
    slots = block_home[neg_ids[0]]
    owner = slots // per_dev // n_fsdp
    local = slots % per_dev
    at_z, at_y = owner // RING, owner % RING
    on_ring = jnp.where(core == 0, at_z, at_y)
    on_row = jnp.where(core == 0, at_y, at_z)
    order = jnp.arange(named)
    earlier = (on_row[None, :] == on_row[:, None]) & (order[None, :] < order[:, None])
    rank = jnp.sum(earlier.astype(jnp.int32), axis=1)
    hit = (on_row[:, None, None] == jnp.arange(RING)[None, :, None]) & (
        rank[:, None, None] == jnp.arange(per_dev)[None, None, :]
    )
    block = on_ring * per_dev + local
    lists = jnp.sum(jnp.where(hit, block[:, None, None] + 1, 0), axis=0) - 1
    lists = jnp.broadcast_to(lists[:, :, None], lists.shape + (128,))

    full_weight, turned, grad_rows, loss_local = embedding_gradients(
        logit_scale, queries, passages, weight, bank, lists
    )
    grad_weight, losses, back_q, back_p = reduce_gradient(turned, grad_rows, full_weight, loss_local)
    loss = losses[0, 0] / (count_q * n_dp * n_fsdp)
    return (loss, grad_weight, back_q, back_p)


def solution(mesh):
    return jax.shard_map(
        body,
        mesh=mesh,
        in_specs=(
            P(("dp", "fsdp"), None),
            P(("dp", "fsdp"), None),
            P("fsdp", None),
            P(("dp", "fsdp"), None, None),
            P(("dp", "fsdp"), None),
            P(),
        ),
        out_specs=(P(), P(("dp", "fsdp"), None), P(("dp", "fsdp"), None), P(("dp", "fsdp"), None)),
        check_vma=False,
    )
```
